32 devices in a mesh: groups: 2 (over x), ctx: 8 (over z, y), dp: 2 (over core).
Axes of the slice: x: 2, y: 2, z: 4, core: 2. Of those that a mesh axis runs over, the one named last changes fastest.
Arguments:
- queries: bfloat16 [4, 2048, 512], P(('groups', 'dp'), 'ctx'), parts along dimension 0, may hold values from -6 to 6
- keys: bfloat16 [4, 2048, 512], P(('groups', 'dp'), 'ctx'), parts along dimension 0, may hold values from -6 to 6
- values: bfloat16 [4, 2048, 512], P(('groups', 'dp'), 'ctx'), parts along dimension 0, may hold values from -6 to 6
- gates: bfloat16 [4, 2048, 512], P(('groups', 'dp'), 'ctx'), parts along dimension 0, may hold values from -6 to 6
- out_weight: bfloat16 [512, 1024], replicated, may hold values from -0.25 to 0.25
- grad_out: bfloat16 [4, 2048, 1024], P(('groups', 'dp'), 'ctx'), parts along dimension 0, may hold values from -6 to 6
- lengths: int32 [4, 4], P(('groups', 'dp')), parts along dimension 0, may hold values from 1 to 1024, 2048 in all within a row
Outputs:
- output: bfloat16 [4, 2048, 1024], P(('groups', 'dp'), 'ctx'), parts along dimension 0
- grad_weight: float32 [1024, 1024], P(('groups', 'ctx', 'dp')), parts along dimension 0
- grad_queries: bfloat16 [4, 2048, 512], P(('groups', 'dp'), 'ctx'), parts along dimension 0
- grad_keys: bfloat16 [4, 2048, 512], P(('groups', 'dp'), 'ctx'), parts along dimension 0
- grad_values: bfloat16 [4, 2048, 512], P(('groups', 'dp'), 'ctx'), parts along dimension 0
- grad_gates: bfloat16 [4, 2048, 512], P(('groups', 'dp'), 'ctx'), parts along dimension 0
The draws below stay inside these ranges and needn't reach their ends.
There are 2 independent parts, one for each index of `groups`. The reference program is written for one: setup_inputs(seed, part) draws one part's arguments, and reference() takes and returns one part's arrays. A program takes and returns all parts, laid end to end along the dimension named above; an argument that names none is the same for every part. Nothing has to cross between parts.
Inputs may be any that keep to these rules, and one draw needn't show every extreme that they name: `lengths`: in each packed row the 4 histories fill all 2048 positions in order, and one is exactly 1024 long.
All inputs are finite; a program needn't handle non-finite values.
Results may differ from the reference program's by a relative error of at most 0.0058.
Values may be sent and summed in bfloat16 or wider, within the bound.
No kernel may reach another device: no remote copies, remote signals or barrier semaphores. Data moves between devices by JAX's collectives and lax.ppermute only.
A program may use at most 128 MiB of HBM per device.

```python
import math
import jax
import jax.numpy as jnp
import numpy as np
from jax import lax

D = 1024
HEAD = 128
HEADS = 4
TOK_DEV = 256
HW = 512
SPAN = 4
MOST_LEN = 1024
TOKENS = 2048
SEQS = 2
USERS = 4


def levels(own_key, shape, split, smallest, high):
    loudness = 1.0
    for position, blocks in split:
        draws = jax.random.uniform(jax.random.fold_in(jax.random.fold_in(own_key, 6), position), (blocks,), jnp.float32, smallest / len(split), high / len(split))
        loudness = loudness * jnp.repeat(jnp.exp(draws), shape[position] // blocks).reshape((-1,) + (1,) * (len(shape) - 1 - position))
    return loudness


def split_up(amount, total, most, skew):
    portions = [(1 << 20) // math.isqrt(grade ** skew) + 1 for grade in range(2, amount + 1)]
    spare, given = total - most - (amount - 1), [1] * (amount - 1)
    while spare > 0:
        movable = [i for i in range(amount - 1) if given[i] < most]
        pool, left = sum([portions[i] for i in movable]), spare
        for i in movable:
            extra = min(most - given[i], max(1, left * portions[i] // pool), spare)
            given[i] = given[i] + extra
            spare = spare - extra
    return np.array([most] + given)


def uneven_parts(key, amount, total, most, skew):
    if amount == 2:
        one = jax.random.randint(key, (), max(1, total - most), min(most, total - 1) + 1)
        return jnp.stack([one, total - one])
    sizes = jnp.asarray(split_up(amount, total, most, skew), jnp.int32)
    pairs = (amount - 1) // 2
    source_of, sink = sizes[1:1 + 2 * pairs:2], sizes[2:2 + 2 * pairs:2]
    room = jnp.minimum(source_of - 1, most - sink)
    passed = jax.random.randint(jax.random.fold_in(key, 1), (pairs,), 0, 1 << 20) % (room + 1)
    sizes = sizes.at[1:1 + 2 * pairs:2].set(source_of - passed).at[2:2 + 2 * pairs:2].set(sink + passed)
    return sizes[jax.random.permutation(jax.random.fold_in(key, 2), amount)]


def centred(rng, dims, scale, most, cuts=(), kind=jnp.bfloat16):
    result = jax.random.normal(rng, dims, jnp.float32) * scale
    if len(cuts) > 0:
        result = levels(rng, dims, cuts, -0.22, 0.18) * result
    return jnp.clip(result, min=-most, max=most).astype(kind)


def setup_inputs(seed: int = 0, part: int = 0) -> dict:
    key_of = jax.random.split(jax.random.key(seed), 8)
    part_keys = jax.random.split(jax.random.fold_in(key_of[7], part), 8)
    return {
        "queries": centred(part_keys[0], (SEQS, TOKENS, HW), 1.0, 6.0, ((0, 2), (1, 8))),
        "keys": centred(part_keys[1], (SEQS, TOKENS, HW), 1.0, 6.0, ((0, 2), (1, 8))),
        "values": centred(part_keys[2], (SEQS, TOKENS, HW), 1.0, 6.0, ((0, 2), (1, 8))),
        "gates": centred(part_keys[3], (SEQS, TOKENS, HW), 1.0, 6.0, ((0, 2), (1, 8))),
        "out_weight": centred(key_of[4], (HW, D), HW ** -0.5, 0.25),
        "grad_out": centred(part_keys[5], (SEQS, TOKENS, D), 1.0, 6.0, ((0, 2), (1, 8))),
        "lengths": jax.vmap(lambda own: uneven_parts(own, USERS, TOKENS, MOST_LEN, 1))(jax.random.split(part_keys[6], SEQS)).reshape((SEQS, USERS)).astype(jnp.int32),
    }


EPS = 1e-05

def silu_slope(score):
    sigma = jax.nn.sigmoid(score)
    return sigma * (1.0 + score * (1.0 - sigma))

def owners(lengths_row, places):
    ends = jnp.cumsum(lengths_row).astype(jnp.int32)
    return lax.optimization_barrier(jnp.sum((places[:, None] >= ends[None, :]).astype(jnp.int32), axis=1)).astype(jnp.int32)

def row_pass(query_rows, key_rows, value_rows, gate_rows, out_weight, out_grad, lengths_row):
    scale = 1.0 / math.sqrt(HEAD)
    reach = SPAN * TOK_DEV
    key_count = reach + TOK_DEV
    blocks = TOKENS // TOK_DEV
    places = jnp.arange(TOKENS, dtype=jnp.int32)
    users = owners(lengths_row, places)
    pad_keys = jnp.concatenate([jnp.zeros((reach, HW), key_rows.dtype), key_rows], 0)
    pad_values = jnp.concatenate([jnp.zeros((reach, HW), value_rows.dtype), value_rows], 0)
    pad_users = jnp.concatenate([jnp.full((reach,), -1, jnp.int32), users], 0)

    def block_data(block):
        start = (block * TOK_DEV).astype(jnp.int32)
        query_block = lax.dynamic_slice_in_dim(query_rows, start, TOK_DEV, 0).reshape(TOK_DEV, HEADS, HEAD).astype(jnp.float32)
        key_block = lax.dynamic_slice_in_dim(pad_keys, start, key_count, 0).reshape(key_count, HEADS, HEAD).astype(jnp.float32)
        value_block = lax.dynamic_slice_in_dim(pad_values, start, key_count, 0).reshape(key_count, HEADS, HEAD).astype(jnp.float32)
        query_users = lax.dynamic_slice_in_dim(users, start, TOK_DEV, 0)
        key_users = lax.dynamic_slice_in_dim(pad_users, start, key_count, 0)
        query_places = start + jnp.arange(TOK_DEV, dtype=jnp.int32)
        key_places = start - reach + jnp.arange(key_count, dtype=jnp.int32)
        live = (key_places[None, :] <= query_places[:, None]) & (query_users[:, None] == key_users[None, :])
        score = jnp.einsum('qhd,khd->hqk', query_block, key_block) * scale
        attend = lax.optimization_barrier(jnp.where(live[None], jax.nn.silu(score), 0.0).astype(jnp.bfloat16))
        return (start, query_block, key_block, value_block, live, score, attend)

    def forward_block(block):
        start, query_block, key_block, value_block, live, score, attend = block_data(block)
        return jnp.einsum('hqk,khd->qhd', attend.astype(jnp.float32), value_block).reshape(TOK_DEV, HW)
    block_ids = jnp.arange(blocks, dtype=jnp.int32)
    mixed = lax.map(forward_block, block_ids).reshape(TOKENS, HW)
    centered = mixed - lax.optimization_barrier(jnp.mean(mixed, axis=1, keepdims=True))
    inverse = lax.rsqrt(lax.optimization_barrier(jnp.mean(centered * centered, axis=1, keepdims=True)) + EPS)
    normed = centered * inverse
    gated = (normed * gate_rows.astype(jnp.float32)).astype(jnp.bfloat16)
    output = jnp.dot(gated, out_weight, preferred_element_type=jnp.float32).astype(jnp.bfloat16)
    weight_term = jnp.dot(gated.T, out_grad, preferred_element_type=jnp.float32)
    grad_gated = jnp.dot(out_grad, out_weight.T, preferred_element_type=jnp.float32)
    grad_gates = (grad_gated * normed).astype(jnp.bfloat16)
    grad_normed = grad_gated * gate_rows.astype(jnp.float32)
    grad_mixed = ((grad_normed - lax.optimization_barrier(jnp.mean(grad_normed, axis=1, keepdims=True)) - normed * lax.optimization_barrier(jnp.mean(grad_normed * normed, axis=1, keepdims=True))) * inverse).astype(jnp.bfloat16)

    def backward_block(carry, block):
        key_total, value_total = carry
        start, query_block, key_block, value_block, live, score, attend = block_data(block)
        grad_block = lax.dynamic_slice_in_dim(grad_mixed, start, TOK_DEV, 0).reshape(TOK_DEV, HEADS, HEAD).astype(jnp.float32)
        value_part = jnp.einsum('hqk,qhd->khd', attend.astype(jnp.float32), grad_block).reshape(key_count, HW)
        slope = jnp.einsum('qhd,khd->hqk', grad_block, value_block)
        score_grad = lax.optimization_barrier(jnp.where(live[None], slope * silu_slope(score), 0.0).astype(jnp.bfloat16)).astype(jnp.float32)
        query_part = (jnp.einsum('hqk,khd->qhd', score_grad, key_block) * scale).reshape(TOK_DEV, HW)
        key_part = (jnp.einsum('hqk,qhd->khd', score_grad, query_block) * scale).reshape(key_count, HW)
        key_total = lax.dynamic_update_slice_in_dim(key_total, lax.dynamic_slice_in_dim(key_total, start, key_count, 0) + key_part, start, 0)
        value_total = lax.dynamic_update_slice_in_dim(value_total, lax.dynamic_slice_in_dim(value_total, start, key_count, 0) + value_part, start, 0)
        return ((key_total, value_total), query_part)
    empty = jnp.zeros((reach + TOKENS, HW), jnp.float32)
    (key_total, value_total), query_parts = lax.scan(backward_block, (empty, empty), block_ids)
    grad_query = query_parts.reshape(TOKENS, HW).astype(jnp.bfloat16)
    grad_key = key_total[reach:].astype(jnp.bfloat16)
    grad_value = value_total[reach:].astype(jnp.bfloat16)
    return (output, weight_term, grad_query, grad_key, grad_value, grad_gates)

def reference(queries, keys, values, gates, out_weight, grad_out, lengths):
    outputs, query_grads, key_grads, value_grads, gate_grads = ([], [], [], [], [])
    weight_total = jnp.zeros((HW, D), jnp.float32)
    for row in range(SEQS):
        output, weight_term, grad_query, grad_key, grad_value, grad_gate = row_pass(queries[row], keys[row], values[row], gates[row], out_weight, grad_out[row], lengths[row])
        outputs.append(output)
        query_grads.append(grad_query)
        key_grads.append(grad_key)
        value_grads.append(grad_value)
        gate_grads.append(grad_gate)
        weight_total = weight_total + weight_term
    grad_weight = weight_total / math.sqrt(SEQS * TOKENS)
    return (jnp.stack(outputs), grad_weight, jnp.stack(query_grads), jnp.stack(key_grads), jnp.stack(value_grads), jnp.stack(gate_grads))
```

```python
import functools
import math

import jax
import jax.numpy as jnp
from jax import lax
from jax.experimental import pallas as pl
from jax.experimental.pallas import tpu as pltpu
from jax.sharding import PartitionSpec as P

HEAD = 128
EPS = 1e-05
SCALE = 1.0 / math.sqrt(HEAD)
BF16 = jnp.bfloat16
F32 = jnp.float32
VMEM = pl.BlockSpec(memory_space=pltpu.VMEM)
SMEM = pl.BlockSpec(memory_space=pltpu.SMEM)


def shifted(block, distance):
    devices = range(lax.axis_size("ctx"))
    return lax.ppermute(block, "ctx", [(i, i + distance) for i in devices if i + distance in devices])


def swapped(block, axis, step):
    return lax.ppermute(block, axis, [(i, i ^ step) for i in range(lax.axis_size(axis))])


def dot(a, b, da, db):
    return lax.dot_general(a, b, (((da,), (db,)), ((), ())), preferred_element_type=F32)


def ends_of(lengths_ref):
    ends, total = [], jnp.int32(0)
    for user in range(lengths_ref.shape[1]):
        total = total + lengths_ref[0, user]
        ends.append(total)
    return ends


def first_place(ends, places):
    first = jnp.zeros_like(places)
    for end in ends:
        first = jnp.where(places >= end, end, first)
    return first


def past_place(ends, places):
    past = jnp.zeros_like(places) + ends[-1]
    for end in ends[-2::-1]:
        past = jnp.where(places < end, end, past)
    return past


def score_parts(a, b):
    half = dot(a, b, 1, 1) * (0.5 * SCALE)
    return half, jnp.tanh(half)


def slopes(half, turn):
    attend = half * turn + half
    return attend, (1.0 + turn) + attend * (1.0 - turn)


def head_columns(width):
    return [slice(h, h + HEAD) for h in range(0, width, HEAD)]


def live_rows(ends, place, tok, distance):
    rows = place + lax.broadcasted_iota(jnp.int32, (tok, tok), 0)
    columns = place - distance * tok + lax.broadcasted_iota(jnp.int32, (tok, tok), 1)
    live = columns >= first_place(ends, rows)
    return live & (columns <= rows) if distance == 0 else live


def live_columns(ends, place, tok, distance):
    rows = place + lax.broadcasted_iota(jnp.int32, (tok, tok), 0)
    columns = place + distance * tok + lax.broadcasted_iota(jnp.int32, (tok, tok), 1)
    live = columns < past_place(ends, rows)
    return live & (columns >= rows) if distance == 0 else live


def mix_kernel(ahead, distances, project, *refs):
    count = len(distances)
    lengths_ref, q_ref = refs[:2]
    k_refs, v_refs = refs[2 : 2 + count], refs[2 + count : 2 + 2 * count]
    mixed_ref = refs[-1]
    if project:
        out_grad_ref, weight_ref, grad_gated_ref, mixed_ref = refs[2 + 2 * count :]
        grad_gated_ref[...] = dot(out_grad_ref[...], weight_ref[...], 1, 1)
    tok, width = q_ref.shape
    place = (lax.axis_index("ctx") + ahead) * tok
    ends = ends_of(lengths_ref)
    for n, distance in enumerate(distances):
        live = live_rows(ends, place, tok, distance)
        for cols in head_columns(width):
            half, turn = score_parts(q_ref[:, cols], k_refs[n][:, cols])
            attend = jnp.where(live, half * turn + half, 0.0).astype(BF16)
            term = dot(attend, v_refs[n][:, cols], 1, 0)
            if n > 0:
                term = term + mixed_ref[:, cols].astype(F32)
            mixed_ref[:, cols] = term.astype(mixed_ref.dtype)


def norm_kernel(near_ref, far_ref, grad_gated_ref, gates_ref, gated_ref, grad_gates_ref, grad_mixed_ref):
    mixed = near_ref[...] + far_ref[...].astype(F32)
    gates = gates_ref[...].astype(F32)
    grad_gated = grad_gated_ref[...]
    centered = mixed - jnp.mean(mixed, axis=1, keepdims=True)
    inverse = lax.rsqrt(jnp.mean(centered * centered, axis=1, keepdims=True) + EPS)
    normed = centered * inverse
    gated_ref[...] = (normed * gates).astype(BF16)
    grad_gates_ref[...] = (grad_gated * normed).astype(BF16)
    grad_normed = grad_gated * gates
    grad_mixed_ref[...] = (
        (
            grad_normed
            - jnp.mean(grad_normed, axis=1, keepdims=True)
            - normed * jnp.mean(grad_normed * normed, axis=1, keepdims=True)
        )
        * inverse
    ).astype(BF16)


def query_grad_kernel(ahead, distances, *refs):
    count = len(distances)
    lengths_ref, q_ref, grad_ref = refs[:3]
    k_refs, v_refs = refs[3 : 3 + count], refs[3 + count : 3 + 2 * count]
    out_ref = refs[-1]
    tok, width = q_ref.shape
    place = (lax.axis_index("ctx") + ahead) * tok
    ends = ends_of(lengths_ref)
    for n, distance in enumerate(distances):
        live = live_rows(ends, place, tok, distance)
        for cols in head_columns(width):
            _, slope = slopes(*score_parts(q_ref[:, cols], k_refs[n][:, cols]))
            pull = dot(grad_ref[:, cols], v_refs[n][:, cols], 1, 1)
            score_grad = jnp.where(live, pull * slope, 0.0).astype(BF16)
            term = dot(score_grad, k_refs[n][:, cols], 1, 0) * (0.5 * SCALE)
            if n > 0:
                term = term + out_ref[:, cols].astype(F32)
            out_ref[:, cols] = term.astype(out_ref.dtype)


def key_grad_kernel(distances, carried, *refs):
    count = len(distances)
    lengths_ref, k_ref, v_ref = refs[:3]
    q_refs, grad_refs = refs[3 : 3 + count], refs[3 + count : 3 + 2 * count]
    key_out, value_out = refs[-2:]
    tok, width = k_ref.shape
    place = lax.axis_index("ctx") * tok
    ends = ends_of(lengths_ref)
    lives = [live_columns(ends, place, tok, distance) for distance in distances]
    for cols in head_columns(width):
        if carried:
            key_grad = refs[3 + 2 * count][:, cols]
            value_grad = refs[4 + 2 * count][:, cols]
        else:
            key_grad = value_grad = jnp.zeros((tok, HEAD), F32)
        for n in range(count):
            attend, slope = slopes(*score_parts(k_ref[:, cols], q_refs[n][:, cols]))
            attend = jnp.where(lives[n], attend, 0.0).astype(BF16)
            value_grad = value_grad + dot(attend, grad_refs[n][:, cols], 1, 0)
            pull = dot(v_ref[:, cols], grad_refs[n][:, cols], 1, 1)
            score_grad = jnp.where(lives[n], pull * slope, 0.0).astype(BF16)
            key_grad = key_grad + dot(score_grad, q_refs[n][:, cols], 1, 0) * (0.5 * SCALE)
        key_out[:, cols] = key_grad.astype(key_out.dtype)
        value_out[:, cols] = value_grad.astype(value_out.dtype)


def out_kernel(gated_ref, weight_ref, out_ref):
    out_ref[...] = dot(gated_ref[...], weight_ref[...], 1, 0).astype(BF16)


def weight_kernel(parts, gated_ref, out_grad_ref, keep_ref, give_ref, total_ref):
    total_ref[...] = dot(gated_ref[...], out_grad_ref[...], 0, 0)
    rows = total_ref.shape[0] // (2 * parts)
    mine = lax.axis_index("dp")
    for part in range(parts):
        to = pl.ds(part * rows, rows)
        keep = pl.multiple_of((2 * part + mine) * rows, rows)
        give = pl.multiple_of((2 * part + 1 - mine) * rows, rows)
        keep_ref[to, :] = total_ref[pl.ds(keep, rows), :]
        give_ref[to, :] = total_ref[pl.ds(give, rows), :].astype(BF16)


def call(kernel, outs, args, flops, scratch=()):
    shapes = [jax.ShapeDtypeStruct(shape, dtype) for shape, dtype in outs]
    moved = sum(math.prod(a.shape) * a.dtype.itemsize for a in [*args, *shapes])
    return pl.pallas_call(
        kernel,
        out_shape=shapes,
        in_specs=[SMEM if a.dtype == jnp.int32 else VMEM for a in args],
        out_specs=[VMEM] * len(shapes),
        scratch_shapes=list(scratch),
        cost_estimate=pl.CostEstimate(flops=flops, bytes_accessed=moved, transcendentals=0),
        compiler_params=pltpu.CompilerParams(vmem_limit_bytes=48 * 1024 * 1024),
    )(*args)


def earlier_blocks(block, most):
    blocks = {0: block}
    even = lax.axis_index("ctx") % 2 == 0
    for distance in range(2, most + 1, 2):
        blocks[distance] = shifted(blocks[distance - 2], 2)
        blocks[distance - 1] = swapped(
            jnp.where(even, blocks[distance - 2], blocks[distance]), "ctx", 1
        )
    return blocks


def later_blocks(block, most):
    blocks = {0: block}
    for distance in range(1, most + 1):
        step = 2 - distance % 2
        blocks[distance] = shifted(blocks[distance - step], -step)
    return blocks


def summed_rows(keep, give):
    count, index = lax.axis_size("ctx"), lax.axis_index("ctx")
    total = keep + swapped(give, "dp", 1).astype(F32)
    step = 1
    while step < count:
        pairs = total.reshape(count // (2 * step), 2, -1, total.shape[-1])
        bit = (index // step) % 2
        give = lax.dynamic_index_in_dim(pairs, 1 - bit, 1, False).astype(BF16)
        keep = lax.dynamic_index_in_dim(pairs, bit, 1, False)
        total = (keep + swapped(give, "ctx", step).astype(F32)).reshape(-1, total.shape[-1])
        step *= 2
    return total


def local(queries, keys, values, gates, out_weight, grad_out, lengths):
    q, k, v, gate_rows, out_grad = queries[0], keys[0], values[0], gates[0], grad_out[0]
    tok, width = q.shape
    model = out_grad.shape[1]
    count = lax.axis_size("ctx")
    reach = min(8, count // 2)
    mid = reach // 2
    pair_flops = 2 * tok * tok * width
    key_at = earlier_blocks(k, mid)
    value_at = earlier_blocks(v, mid)
    query_at = later_blocks(q, reach)

    near = list(range(mid + 1))
    back = list(range(1, mid + 1))
    far = [mid + d for d in back]
    (far_term,) = call(
        functools.partial(mix_kernel, mid, far, False),
        [((tok, width), BF16)],
        [lengths, query_at[mid], *[key_at[d] for d in back], *[value_at[d] for d in back]],
        2 * pair_flops * len(back),
    )
    far_mixed = shifted(far_term, mid)
    grad_gated, near_mixed = call(
        functools.partial(mix_kernel, 0, near, True),
        [((tok, width), F32), ((tok, width), F32)],
        [lengths, q, *[key_at[d] for d in near], *[value_at[d] for d in near], out_grad, out_weight],
        2 * pair_flops * len(near) + 2 * tok * width * model,
    )
    gated, grad_gates, grad_mixed = call(
        norm_kernel,
        [((tok, width), BF16)] * 3,
        [near_mixed, far_mixed, grad_gated, gate_rows],
        20 * tok * width,
    )
    grad_at = later_blocks(grad_mixed, reach)
    keep, give = call(
        functools.partial(weight_kernel, count),
        [((width // 2, model), F32), ((width // 2, model), BF16)],
        [gated, out_grad],
        2 * tok * width * model,
        [pltpu.VMEM((width, model), F32)],
    )
    (output,) = call(
        out_kernel, [((tok, model), BF16)], [gated, out_weight], 2 * tok * width * model
    )
    (far_query_term,) = call(
        functools.partial(query_grad_kernel, mid, far),
        [((tok, width), BF16)],
        [lengths, query_at[mid], grad_at[mid], *[key_at[d] for d in back], *[value_at[d] for d in back]],
        3 * pair_flops * len(back),
    )
    far_query = shifted(far_query_term, mid)
    (near_query,) = call(
        functools.partial(query_grad_kernel, 0, near),
        [((tok, width), F32)],
        [lengths, q, grad_mixed, *[key_at[d] for d in near], *[value_at[d] for d in near]],
        3 * pair_flops * len(near),
    )
    key_part, value_part = call(
        functools.partial(key_grad_kernel, near, False),
        [((tok, width), F32)] * 2,
        [lengths, k, v, *[query_at[d] for d in near], *[grad_at[d] for d in near]],
        4 * pair_flops * len(near),
    )
    key_grad, value_grad = call(
        functools.partial(key_grad_kernel, far, True),
        [((tok, width), BF16)] * 2,
        [lengths, k, v, *[query_at[d] for d in far], *[grad_at[d] for d in far], key_part, value_part],
        4 * pair_flops * len(far),
    )
    query_grad = (near_query + far_query.astype(F32)).astype(BF16)
    total_rows = lax.axis_size("dp") * count * tok
    grad_weight = summed_rows(keep, give) / math.sqrt(total_rows)
    return (
        output[None],
        grad_weight,
        query_grad[None],
        key_grad[None],
        value_grad[None],
        grad_gates[None],
    )


def solution(mesh):
    rows = P(("groups", "dp"), "ctx", None)
    in_specs = (rows, rows, rows, rows, P(), rows, P(("groups", "dp"), None))
    out_specs = (rows, P(("groups", "ctx", "dp"), None), rows, rows, rows, rows)
    return jax.shard_map(local, mesh=mesh, in_specs=in_specs, out_specs=out_specs, check_vma=False)
```

```python
import functools
import math

import jax
import jax.numpy as jnp
from jax import lax
from jax.experimental import pallas as pl
from jax.experimental.pallas import tpu as pltpu
from jax.sharding import PartitionSpec as P

HEAD = 128
EPS = 1e-05
SCALE = 1.0 / math.sqrt(HEAD)
BF16 = jnp.bfloat16
F32 = jnp.float32
VMEM = pl.BlockSpec(memory_space=pltpu.VMEM)
ANY = pl.BlockSpec(memory_space=pl.ANY)


def shifted(block, distance):
    devices = range(lax.axis_size("ctx"))
    return lax.ppermute(block, "ctx", [(i, i + distance) for i in devices if i + distance in devices])


def swapped(block, axis, step):
    return lax.ppermute(block, axis, [(i, i ^ step) for i in range(lax.axis_size(axis))])


def dot(a, b, da, db):
    return lax.dot_general(a, b, (((da,), (db,)), ((), ())), preferred_element_type=F32)


def ends_of(lengths_ref):
    ends, total = [], jnp.int32(0)
    for user in range(lengths_ref.shape[1]):
        total = total + lengths_ref[0, user]
        ends.append(total)
    return ends


def first_place(ends, places):
    first = jnp.zeros_like(places)
    for end in ends:
        first = jnp.where(places >= end, end, first)
    return first


def past_place(ends, places):
    past = jnp.zeros_like(places) + ends[-1]
    for end in ends[-2::-1]:
        past = jnp.where(places < end, end, past)
    return past


def crossing(ends, place, distance, tok):
    return first_place(ends, place) - (place - distance * tok), past_place(ends, place) - place


def own_mask(ends, place, tok, transposed):
    rows = place + lax.broadcasted_iota(jnp.int32, (tok, tok), 0)
    columns = place + lax.broadcasted_iota(jnp.int32, (tok, tok), 1)
    ids = place + lax.broadcasted_iota(jnp.int32, (tok, 1), 0)
    if transposed:
        return (columns >= rows) & (columns < past_place(ends, ids))
    return (columns <= rows) & (columns >= first_place(ends, ids))


def row_numbers(tok):
    return lax.broadcasted_iota(jnp.int32, (tok, HEAD), 0)


def half_scores(a, b):
    return dot(a, b, 1, 1) * (0.5 * SCALE)


def silu(half):
    return half * jnp.tanh(half) + half


def slopes(half):
    turn = jnp.tanh(half)
    attend = half * turn + half
    return attend, (1.0 + turn) + attend * (1.0 - turn)


def staggered(width, begin, finish):
    heads = [slice(h, h + HEAD) for h in range(0, width, HEAD)]
    begun = begin(heads[0])
    for now, after in zip(heads, heads[1:] + [None]):
        ready = begun
        if after is not None:
            begun = begin(after)
        finish(now, ready)


def mix_kernel(ahead, distances, project, *refs):
    count = len(distances)
    lengths_ref, q_ref = refs[:2]
    k_refs, v_refs = refs[2 : 2 + count], refs[2 + count : 2 + 2 * count]
    mixed_ref, total_ref = refs[-2:]
    if project:
        out_grad_ref, weight_ref, grad_gated_ref, total_ref = refs[2 + 2 * count :]
        grad_gated_ref[...] = dot(out_grad_ref[...], weight_ref[...], 1, 1)
    tok, width = q_ref.shape
    place = (lax.axis_index("ctx") + ahead) * tok
    ends = ends_of(lengths_ref)

    def pair(k_ref, v_ref, mask, dead, alive):
        def finish(cols, half):
            attend = silu(half)
            if mask is not None:
                total_ref[:, cols] = dot(jnp.where(mask, attend, 0.0).astype(BF16), v_ref[:, cols], 1, 0)
                return
            number = row_numbers(tok)
            v = jnp.where(number >= dead, v_ref[:, cols], 0.0).astype(BF16)
            term = dot(attend.astype(BF16), v, 1, 0)
            total_ref[:, cols] += jnp.where(number < alive, term, 0.0)

        staggered(width, lambda cols: half_scores(q_ref[:, cols], k_ref[:, cols]), finish)

    if distances[0] > 0:
        total_ref[...] = jnp.zeros_like(total_ref)
    for n, distance in enumerate(distances):
        if distance == 0:
            pair(k_refs[n], v_refs[n], own_mask(ends, place, tok, False), None, None)
        else:
            dead, alive = crossing(ends, place, distance, tok)
            pl.when(dead < tok)(functools.partial(pair, k_refs[n], v_refs[n], None, dead, alive))
    if not project:
        mixed_ref[...] = total_ref[...].astype(BF16)


def norm_kernel(near_ref, far_ref, grad_gated_ref, gates_ref, gated_ref, grad_gates_ref, grad_mixed_ref):
    mixed = near_ref[...] + far_ref[...].astype(F32)
    gates = gates_ref[...].astype(F32)
    grad_gated = grad_gated_ref[...]
    centered = mixed - jnp.mean(mixed, axis=1, keepdims=True)
    inverse = lax.rsqrt(jnp.mean(centered * centered, axis=1, keepdims=True) + EPS)
    normed = centered * inverse
    gated_ref[...] = (normed * gates).astype(BF16)
    grad_gates_ref[...] = (grad_gated * normed).astype(BF16)
    grad_normed = grad_gated * gates
    grad_mixed_ref[...] = (
        (
            grad_normed
            - jnp.mean(grad_normed, axis=1, keepdims=True)
            - normed * jnp.mean(grad_normed * normed, axis=1, keepdims=True)
        )
        * inverse
    ).astype(BF16)


def query_grad_kernel(ahead, distances, *refs):
    count = len(distances)
    lengths_ref, q_ref, grad_ref = refs[:3]
    k_refs, v_refs = refs[3 : 3 + count], refs[3 + count : 3 + 2 * count]
    out_ref, total_ref = refs[-2:]
    tok, width = q_ref.shape
    place = (lax.axis_index("ctx") + ahead) * tok
    ends = ends_of(lengths_ref)

    def pair(k_ref, v_ref, mask, dead, alive):
        def begin(cols):
            return half_scores(q_ref[:, cols], k_ref[:, cols]), dot(grad_ref[:, cols], v_ref[:, cols], 1, 1)

        def finish(cols, begun):
            half, pull = begun
            score_grad = pull * slopes(half)[1]
            if mask is not None:
                total_ref[:, cols] = dot(jnp.where(mask, score_grad, 0.0).astype(BF16), k_ref[:, cols], 1, 0)
                return
            number = row_numbers(tok)
            k = jnp.where(number >= dead, k_ref[:, cols], 0.0).astype(BF16)
            term = dot(score_grad.astype(BF16), k, 1, 0)
            total_ref[:, cols] += jnp.where(number < alive, term, 0.0)

        staggered(width, begin, finish)

    if distances[0] > 0:
        total_ref[...] = jnp.zeros_like(total_ref)
    for n, distance in enumerate(distances):
        if distance == 0:
            pair(k_refs[n], v_refs[n], own_mask(ends, place, tok, False), None, None)
        else:
            dead, alive = crossing(ends, place, distance, tok)
            pl.when(dead < tok)(functools.partial(pair, k_refs[n], v_refs[n], None, dead, alive))
    total = total_ref[...] * (0.5 * SCALE)
    out_ref[...] = total.astype(out_ref.dtype)


def key_grad_kernel(distances, last, *refs):
    count = len(distances)
    lengths_ref, k_ref, v_ref = refs[:3]
    q_refs, grad_refs = refs[3 : 3 + count], refs[3 + count : 3 + 2 * count]
    key_out, value_out, key_total, value_total = refs[-4:] if last else refs[-2:] * 2
    tok, width = k_ref.shape
    place = lax.axis_index("ctx") * tok
    ends = ends_of(lengths_ref)

    def pair(q_ref, grad_ref, mask, dead, alive):
        def begin(cols):
            return half_scores(k_ref[:, cols], q_ref[:, cols]), dot(v_ref[:, cols], grad_ref[:, cols], 1, 1)

        def finish(cols, begun):
            half, pull = begun
            attend, slope = slopes(half)
            score_grad = pull * slope
            if mask is not None:
                value_total[:, cols] = dot(jnp.where(mask, attend, 0.0).astype(BF16), grad_ref[:, cols], 1, 0)
                key_total[:, cols] = dot(jnp.where(mask, score_grad, 0.0).astype(BF16), q_ref[:, cols], 1, 0)
                return
            number = row_numbers(tok)
            grad = jnp.where(number < alive, grad_ref[:, cols], 0.0).astype(BF16)
            q = jnp.where(number < alive, q_ref[:, cols], 0.0).astype(BF16)
            value_term = dot(attend.astype(BF16), grad, 1, 0)
            key_term = dot(score_grad.astype(BF16), q, 1, 0)
            value_total[:, cols] += jnp.where(number >= dead, value_term, 0.0)
            key_total[:, cols] += jnp.where(number >= dead, key_term, 0.0)

        staggered(width, begin, finish)

    if distances[0] > 0:
        key_total[...] = refs[3 + 2 * count][...]
        value_total[...] = refs[4 + 2 * count][...]
    for n, distance in enumerate(distances):
        if distance == 0:
            pair(q_refs[n], grad_refs[n], own_mask(ends, place, tok, True), None, None)
        else:
            dead, alive = crossing(ends, place + distance * tok, distance, tok)
            pl.when(dead < tok)(functools.partial(pair, q_refs[n], grad_refs[n], None, dead, alive))
    if last:
        key_out[...] = (key_total[...] * (0.5 * SCALE)).astype(BF16)
        value_out[...] = value_total[...].astype(BF16)


def parted(total, bit, keep_ref, give_ref):
    for part in range(keep_ref.shape[0]):
        keep_ref[part] = total(2 * part + bit)
        give_ref[part] = total(2 * part + 1 - bit).astype(BF16)


def out_kernel(gated_ref, weight_ref, out_ref):
    out_ref[...] = dot(gated_ref[...], weight_ref[...], 1, 0).astype(BF16)


def weight_kernel(gated_ref, out_grad_ref, keep_ref, give_ref, total_ref):
    total_ref[...] = dot(gated_ref[...], out_grad_ref[...], 0, 0)
    rows = keep_ref.shape[1]
    parted(
        lambda chunk: total_ref[pl.ds(pl.multiple_of(chunk * rows, rows), rows), :],
        lax.axis_index("dp"),
        keep_ref,
        give_ref,
    )


def part_kernel(step, kept_ref, came_ref, keep_ref, give_ref):
    parted(
        lambda chunk: kept_ref[chunk] + came_ref[chunk].astype(F32),
        (lax.axis_index("ctx") // step) % 2,
        keep_ref,
        give_ref,
    )


def last_part_kernel(factor, kept_ref, came_ref, out_ref):
    out_ref[...] = (kept_ref[0] + came_ref[0].astype(F32)) * factor


def add_kernel(a_ref, b_ref, out_ref):
    out_ref[...] = (a_ref[...] + b_ref[...].astype(F32)).astype(out_ref.dtype)


def pick_kernel(even_ref, odd_ref, out_ref):
    even = lax.axis_index("ctx") % 2 == 0

    @pl.when(even)
    def _():
        out_ref[...] = even_ref[...]

    @pl.when(jnp.logical_not(even))
    def _():
        out_ref[...] = odd_ref[...]


def call(kernel, outs, args, micros, scratch=(), after=()):
    held = len(args)

    def body(*refs):
        kernel(*refs[:held], *refs[held + len(after) :])

    shapes = [jax.ShapeDtypeStruct(shape, dtype) for shape, dtype in outs]
    return pl.pallas_call(
        body,
        out_shape=shapes,
        in_specs=[VMEM] * len(args) + [ANY] * len(after),
        out_specs=[VMEM] * len(shapes),
        scratch_shapes=list(scratch),
        cost_estimate=pl.CostEstimate(flops=int(micros * 1.0e6), bytes_accessed=0, transcendentals=0),
        compiler_params=pltpu.CompilerParams(vmem_limit_bytes=48 * 1024 * 1024),
    )(*args, *after)


def picked(even_sends, odd_sends, after=()):
    (sent,) = call(
        pick_kernel, [(even_sends.shape, even_sends.dtype)], [even_sends, odd_sends], 0.2, (), after
    )
    return sent


def exchanged(even_sends, odd_sends):
    return swapped(picked(even_sends, odd_sends), "ctx", 1)


def earlier_blocks(block, most):
    blocks = {0: block}
    for distance in range(2, most + 1, 2):
        blocks[distance] = shifted(blocks[distance - 2], 2)
        blocks[distance - 1] = exchanged(blocks[distance - 2], blocks[distance])
    return blocks


def later_blocks(block, most):
    blocks = {0: block}
    for distance in range(2, most + 1, 2):
        blocks[distance] = shifted(blocks[distance - 2], -2)
    for distance in range(1, most, 2):
        blocks[distance] = exchanged(blocks[distance + 1], blocks[distance - 1])
    return blocks


def local(queries, keys, values, gates, out_weight, grad_out, lengths):
    q, k, v, gate_rows, out_grad = queries[0], keys[0], values[0], gates[0], grad_out[0]
    tok, width = q.shape
    model = out_grad.shape[1]
    count, cores = lax.axis_size("ctx"), lax.axis_size("dp")
    reach = min(8, count // 2)
    mid = reach // 2
    one, wide = [((tok, width), BF16)], [((tok, width), F32)]
    total = pltpu.VMEM((tok, width), F32)
    key_at = earlier_blocks(k, mid)
    value_at = earlier_blocks(v, mid)
    query_at = {0: q}
    for distance in range(2, reach + 1, 2):
        query_at[distance] = shifted(query_at[distance - 2], -2)

    near = list(range(mid + 1))
    back = list(range(1, mid + 1))
    far = [mid + d for d in back]
    back_keys = [key_at[d] for d in back] + [value_at[d] for d in back]
    near_keys = [key_at[d] for d in near] + [value_at[d] for d in near]
    (far_term,) = call(
        functools.partial(mix_kernel, mid, far, False),
        one,
        [lengths, query_at[mid], *back_keys],
        1.0,
        [total],
    )
    far_mixed = shifted(far_term, mid)
    sent = {d: picked(query_at[d + 1], query_at[d - 1], [far_term]) for d in range(1, reach, 2)}
    for distance, block in sent.items():
        query_at[distance] = swapped(block, "ctx", 1)
    grad_gated, near_mixed = call(
        functools.partial(mix_kernel, 0, near, True),
        wide * 2,
        [lengths, q, *near_keys, out_grad, out_weight],
        2.0,
        (),
        list(sent.values()),
    )
    gated, grad_gates, grad_mixed = call(
        norm_kernel,
        one * 3,
        [near_mixed, far_mixed, grad_gated, gate_rows],
        1.0,
    )
    grad_at = later_blocks(grad_mixed, reach)
    chunk = (width // (count * cores), model)
    keep, give = call(
        weight_kernel,
        [((count, *chunk), F32), ((count, *chunk), BF16)],
        [gated, out_grad],
        1.5,
        [pltpu.VMEM((width, model), F32)],
    )
    (output,) = call(out_kernel, [((tok, model), BF16)], [gated, out_weight], 1.0)
    came = swapped(give, "dp", 1)
    arrived = [came]
    step = 1
    while step < count:
        parts = (count // (2 * step), *chunk)
        keep, give = call(
            functools.partial(part_kernel, step),
            [(parts, F32), (parts, BF16)],
            [keep, came],
            0.8,
            (),
            [query_at[1]] if step == 1 else (),
        )
        came = swapped(give, "ctx", step)
        arrived.append(came)
        step *= 2
    (grad_weight,) = call(
        functools.partial(last_part_kernel, 1.0 / math.sqrt(cores * count * tok)),
        [(chunk, F32)],
        [keep, came],
        0.5,
    )
    (near_query,) = call(
        functools.partial(query_grad_kernel, 0, near),
        wide,
        [lengths, q, grad_mixed, *near_keys],
        2.5,
        [total],
    )
    (far_query_term,) = call(
        functools.partial(query_grad_kernel, mid, far),
        one,
        [lengths, query_at[mid], grad_at[mid], *back_keys],
        1.5,
        [total],
        [near_query, output, keep, *[query_at[d] for d in far]],
    )
    far_query = shifted(far_query_term, mid)
    grads = ()
    groups = [
        [d for d in near if d % 2 == 0],
        [d for d in near if d % 2 == 1] + [d for d in far if d % 2 == 0],
        [d for d in far if d % 2 == 1],
    ]
    for n, group in enumerate(groups):
        last = n == len(groups) - 1
        grads = call(
            functools.partial(key_grad_kernel, group, last),
            (one if last else wide) * 2,
            [lengths, k, v, *[query_at[d] for d in group], *[grad_at[d] for d in group], *grads],
            len(group) * 0.9,
            [total] * 2 if last else (),
            arrived[1:2] if n == 1 else (),
        )
    key_grad, value_grad = grads
    (query_grad,) = call(add_kernel, one, [near_query, far_query], 0.3)
    return (
        output[None],
        grad_weight,
        query_grad[None],
        key_grad[None],
        value_grad[None],
        grad_gates[None],
    )


def solution(mesh):
    rows = P(("groups", "dp"), "ctx", None)
    in_specs = (rows, rows, rows, rows, P(), rows, P(("groups", "dp"), None))
    out_specs = (rows, P(("groups", "ctx", "dp"), None), rows, rows, rows, rows)
    return jax.shard_map(local, mesh=mesh, in_specs=in_specs, out_specs=out_specs, check_vma=False)
```

```python
import functools
import math

import jax
import jax.numpy as jnp
from jax import lax
from jax.experimental import pallas as pl
from jax.experimental.pallas import tpu as pltpu
from jax.sharding import PartitionSpec as P

HEAD = 128
EPS = 1e-05
SCALE = 1.0 / math.sqrt(HEAD)
BF16 = jnp.bfloat16
F32 = jnp.float32
VMEM = pl.BlockSpec(memory_space=pltpu.VMEM)
HINT = {
    "pick": 0.001,
    "attend": 0.001,
    "far_mix": 0.001,
    "near_mix": 0.001,
    "norm": 0.001,
    "near_query": 0.001,
    "weight": 0.001,
    "out": 0.001,
    "part": 0.001,
    "sum": 0.001,
    "far_query": 0.001,
    "keys": (0.001, 0.001, 4.0, 0.001),
}
ANY = pl.BlockSpec(memory_space=pl.ANY)


def shifted(block, distance):
    devices = range(lax.axis_size("ctx"))
    return lax.ppermute(block, "ctx", [(i, i + distance) for i in devices if i + distance in devices])


def swapped(block, axis, step):
    return lax.ppermute(block, axis, [(i, i ^ step) for i in range(lax.axis_size(axis))])


def dot(a, b, da, db):
    return lax.dot_general(a, b, (((da,), (db,)), ((), ())), preferred_element_type=F32)


def ends_of(lengths_ref):
    ends, total = [], jnp.int32(0)
    for user in range(lengths_ref.shape[1]):
        total = total + lengths_ref[0, user]
        ends.append(total)
    return ends


def first_place(ends, places):
    first = jnp.zeros_like(places)
    for end in ends:
        first = jnp.where(places >= end, end, first)
    return first


def past_place(ends, places):
    past = jnp.zeros_like(places) + ends[-1]
    for end in ends[-2::-1]:
        past = jnp.where(places < end, end, past)
    return past


def crossing(ends, place, distance, tok):
    return first_place(ends, place) - (place - distance * tok), past_place(ends, place) - place


def own_mask(ends, place, tok, transposed):
    rows = place + lax.broadcasted_iota(jnp.int32, (tok, tok), 0)
    columns = place + lax.broadcasted_iota(jnp.int32, (tok, tok), 1)
    ids = place + lax.broadcasted_iota(jnp.int32, (tok, 1), 0)
    if transposed:
        return (columns >= rows) & (columns < past_place(ends, ids))
    return (columns <= rows) & (columns >= first_place(ends, ids))


def row_numbers(tok):
    return lax.broadcasted_iota(jnp.int32, (tok, HEAD), 0)


def half_scores(a, b):
    return dot(a, b, 1, 1) * (0.5 * SCALE)


def silu(half):
    return half * jnp.tanh(half) + half


def slopes(half):
    turn = jnp.tanh(half)
    attend = half * turn + half
    return attend, (1.0 + turn) + attend * (1.0 - turn)


def staggered(width, begin, finish):
    heads = [slice(h, h + HEAD) for h in range(0, width, HEAD)]
    begun = begin(heads[0])
    for now, after in zip(heads, heads[1:] + [None]):
        ready = begun
        if after is not None:
            begun = begin(after)
        finish(now, ready)


def mix_kernel(distances, *refs):
    count = len(distances)
    lengths_ref, q_ref = refs[:2]
    k_refs, v_refs = refs[2 : 2 + count], refs[2 + count : 2 + 2 * count]
    out_grad_ref, weight_ref, grad_gated_ref, total_ref = refs[2 + 2 * count :]
    grad_gated_ref[...] = dot(out_grad_ref[...], weight_ref[...], 1, 1)
    tok, width = q_ref.shape
    place = lax.axis_index("ctx") * tok
    ends = ends_of(lengths_ref)

    def pair(k_ref, v_ref, mask, dead, alive):
        def finish(cols, half):
            attend = silu(half)
            if mask is not None:
                total_ref[:, cols] = dot(jnp.where(mask, attend, 0.0).astype(BF16), v_ref[:, cols], 1, 0)
                return
            number = row_numbers(tok)
            v = jnp.where(number >= dead, v_ref[:, cols], 0.0).astype(BF16)
            term = dot(attend.astype(BF16), v, 1, 0)
            total_ref[:, cols] += jnp.where(number < alive, term, 0.0)

        staggered(width, lambda cols: half_scores(q_ref[:, cols], k_ref[:, cols]), finish)

    for n, distance in enumerate(distances):
        if distance == 0:
            pair(k_refs[n], v_refs[n], own_mask(ends, place, tok, False), None, None)
        else:
            dead, alive = crossing(ends, place, distance, tok)
            pl.when(dead < tok)(functools.partial(pair, k_refs[n], v_refs[n], None, dead, alive))


def attend_kernel(ahead, distances, *refs):
    lengths_ref, q_ref = refs[:2]
    attend_ref = refs[-1]
    tok, width = q_ref.shape
    heads = width // HEAD
    place = (lax.axis_index("ctx") + ahead) * tok
    ends = ends_of(lengths_ref)
    for n, distance in enumerate(distances):
        dead, alive = crossing(ends, place, distance, tok)

        @pl.when(dead < tok)
        def _(n=n, dead=dead, alive=alive):
            number = row_numbers(tok)

            def begin(cols):
                q = jnp.where(number < alive, q_ref[:, cols], 0.0).astype(BF16)
                return half_scores(q, jnp.where(number >= dead, refs[2 + n][:, cols], 0.0).astype(BF16))

            def finish(cols, half):
                attend_ref[n * heads + cols.start // HEAD] = silu(half).astype(BF16)

            staggered(width, begin, finish)


def far_kernel(ahead, distances, *refs):
    lengths_ref, attend_ref = refs[:2]
    mixed_ref, total_ref = refs[-2:]
    tok, width = mixed_ref.shape
    heads = width // HEAD
    place = (lax.axis_index("ctx") + ahead) * tok
    ends = ends_of(lengths_ref)
    total_ref[...] = jnp.zeros_like(total_ref)
    for n, distance in enumerate(distances):
        dead, _ = crossing(ends, place, distance, tok)

        @pl.when(dead < tok)
        def _(n=n):
            for head in range(heads):
                cols = slice(head * HEAD, (head + 1) * HEAD)
                total_ref[:, cols] += dot(attend_ref[n * heads + head], refs[2 + n][:, cols], 1, 0)

    mixed_ref[...] = total_ref[...].astype(BF16)


def norm_kernel(near_ref, far_ref, grad_gated_ref, gates_ref, gated_ref, normed_ref, grad_mixed_ref):
    mixed = near_ref[...] + far_ref[...].astype(F32)
    gates = gates_ref[...].astype(F32)
    grad_gated = grad_gated_ref[...]
    centered = mixed - jnp.mean(mixed, axis=1, keepdims=True)
    inverse = lax.rsqrt(jnp.mean(centered * centered, axis=1, keepdims=True) + EPS)
    normed = centered * inverse
    gated_ref[...] = (normed * gates).astype(BF16)
    normed_ref[...] = normed
    grad_normed = grad_gated * gates
    grad_mixed_ref[...] = (
        (
            grad_normed
            - jnp.mean(grad_normed, axis=1, keepdims=True)
            - normed * jnp.mean(grad_normed * normed, axis=1, keepdims=True)
        )
        * inverse
    ).astype(BF16)


def query_grad_kernel(ahead, distances, *refs):
    count = len(distances)
    lengths_ref, q_ref, grad_ref = refs[:3]
    k_refs, v_refs = refs[3 : 3 + count], refs[3 + count : 3 + 2 * count]
    out_ref, total_ref = refs[-2:]
    tok, width = q_ref.shape
    place = (lax.axis_index("ctx") + ahead) * tok
    ends = ends_of(lengths_ref)

    def pair(k_ref, v_ref, mask, dead, alive):
        def begin(cols):
            return half_scores(q_ref[:, cols], k_ref[:, cols]), dot(grad_ref[:, cols], v_ref[:, cols], 1, 1)

        def finish(cols, begun):
            half, pull = begun
            score_grad = pull * slopes(half)[1]
            if mask is not None:
                total_ref[:, cols] = dot(jnp.where(mask, score_grad, 0.0).astype(BF16), k_ref[:, cols], 1, 0)
                return
            number = row_numbers(tok)
            k = jnp.where(number >= dead, k_ref[:, cols], 0.0).astype(BF16)
            term = dot(score_grad.astype(BF16), k, 1, 0)
            total_ref[:, cols] += jnp.where(number < alive, term, 0.0)

        staggered(width, begin, finish)

    if distances[0] > 0:
        total_ref[...] = jnp.zeros_like(total_ref)
    for n, distance in enumerate(distances):
        if distance == 0:
            pair(k_refs[n], v_refs[n], own_mask(ends, place, tok, False), None, None)
        else:
            dead, alive = crossing(ends, place, distance, tok)
            pl.when(dead < tok)(functools.partial(pair, k_refs[n], v_refs[n], None, dead, alive))
    total = total_ref[...] * (0.5 * SCALE)
    out_ref[...] = total.astype(out_ref.dtype)


def key_grad_kernel(distances, last, *refs):
    count = len(distances)
    lengths_ref, k_ref, v_ref = refs[:3]
    q_refs, grad_refs = refs[3 : 3 + count], refs[3 + count : 3 + 2 * count]
    if last:
        near_ref, far_ref, key_out, value_out, query_out, key_total, value_total = refs[-7:]
        query_out[...] = (near_ref[...] + far_ref[...].astype(F32)).astype(BF16)
    else:
        key_total, value_total = refs[-2:]
    tok, width = k_ref.shape
    place = lax.axis_index("ctx") * tok
    ends = ends_of(lengths_ref)

    def pair(q_ref, grad_ref, mask, dead, alive):
        def begin(cols):
            return half_scores(k_ref[:, cols], q_ref[:, cols]), dot(v_ref[:, cols], grad_ref[:, cols], 1, 1)

        def finish(cols, begun):
            half, pull = begun
            attend, slope = slopes(half)
            score_grad = pull * slope
            if mask is not None:
                value_total[:, cols] = dot(jnp.where(mask, attend, 0.0).astype(BF16), grad_ref[:, cols], 1, 0)
                key_total[:, cols] = dot(jnp.where(mask, score_grad, 0.0).astype(BF16), q_ref[:, cols], 1, 0)
                return
            number = row_numbers(tok)
            grad = jnp.where(number < alive, grad_ref[:, cols], 0.0).astype(BF16)
            q = jnp.where(number < alive, q_ref[:, cols], 0.0).astype(BF16)
            value_term = dot(attend.astype(BF16), grad, 1, 0)
            key_term = dot(score_grad.astype(BF16), q, 1, 0)
            value_total[:, cols] += jnp.where(number >= dead, value_term, 0.0)
            key_total[:, cols] += jnp.where(number >= dead, key_term, 0.0)

        staggered(width, begin, finish)

    if distances[0] > 0:
        key_total[...] = refs[3 + 2 * count][...]
        value_total[...] = refs[4 + 2 * count][...]
    for n, distance in enumerate(distances):
        if distance == 0:
            pair(q_refs[n], grad_refs[n], own_mask(ends, place, tok, True), None, None)
        else:
            dead, alive = crossing(ends, place + distance * tok, distance, tok)
            pl.when(dead < tok)(functools.partial(pair, q_refs[n], grad_refs[n], None, dead, alive))
    if last:
        key_out[...] = (key_total[...] * (0.5 * SCALE)).astype(BF16)
        value_out[...] = value_total[...].astype(BF16)


def parted(total, bit, keep_ref, give_ref):
    for part in range(keep_ref.shape[0]):
        keep_ref[part] = total(2 * part + bit)
        give_ref[part] = total(2 * part + 1 - bit).astype(BF16)


def out_kernel(gated_ref, weight_ref, grad_gated_ref, normed_ref, out_ref, grad_gates_ref):
    grad_gates_ref[...] = (grad_gated_ref[...] * normed_ref[...]).astype(BF16)
    out_ref[...] = dot(gated_ref[...], weight_ref[...], 1, 0).astype(BF16)


def weight_kernel(gated_ref, out_grad_ref, keep_ref, give_ref, total_ref):
    total_ref[...] = dot(gated_ref[...], out_grad_ref[...], 0, 0)
    rows = keep_ref.shape[1]
    parted(
        lambda chunk: total_ref[pl.ds(pl.multiple_of(chunk * rows, rows), rows), :],
        lax.axis_index("dp"),
        keep_ref,
        give_ref,
    )


def part_kernel(step, kept_ref, came_ref, keep_ref, give_ref):
    parted(
        lambda chunk: kept_ref[chunk] + came_ref[chunk].astype(F32),
        (lax.axis_index("ctx") // step) % 2,
        keep_ref,
        give_ref,
    )


def spread_kernel(step, kept_ref, came_ref, keep_ref, *give_refs):
    own = lax.axis_index("ctx") // step
    keep_ref[0] = kept_ref[own] + came_ref[own].astype(F32)
    for n, give_ref in enumerate(give_refs):
        chunk = own ^ (n + 1)
        give_ref[0] = (kept_ref[chunk] + came_ref[chunk].astype(F32)).astype(BF16)


def sum_kernel(factor, kept_ref, *refs):
    rows = kept_ref[0]
    for came_ref in refs[:-2]:
        rows = rows + came_ref[0].astype(F32)
    out_ref, mark_ref = refs[-2:]
    out_ref[...] = rows * factor
    mark_ref[...] = jnp.zeros_like(mark_ref)


def pick_kernel(even_ref, odd_ref, out_ref):
    even = lax.axis_index("ctx") % 2 == 0

    @pl.when(even)
    def _():
        out_ref[...] = even_ref[...]

    @pl.when(jnp.logical_not(even))
    def _():
        out_ref[...] = odd_ref[...]


def pick_far_kernel(odd_ref, even_ref, out_ref, sem):
    even = lax.axis_index("ctx") % 2 == 0

    @pl.when(even)
    def _():
        copy = pltpu.make_async_copy(even_ref, out_ref, sem)
        copy.start()
        copy.wait()

    @pl.when(jnp.logical_not(even))
    def _():
        out_ref[...] = odd_ref[...]


def call(kernel, outs, args, micros, scratch=(), after=()):
    held = len(args)

    def body(*refs):
        kernel(*refs[:held], *refs[held + len(after) :])

    if kernel is pick_far_kernel:
        body = kernel

    shapes = [jax.ShapeDtypeStruct(shape, dtype) for shape, dtype in outs]
    return pl.pallas_call(
        body,
        out_shape=shapes,
        in_specs=[VMEM] * len(args) + [ANY] * len(after),
        out_specs=[VMEM] * len(shapes),
        scratch_shapes=list(scratch),
        cost_estimate=pl.CostEstimate(flops=int(micros * 1.1535e9), bytes_accessed=0, transcendentals=0),
        compiler_params=pltpu.CompilerParams(vmem_limit_bytes=48 * 1024 * 1024),
    )(*args, *after)


def picked(even_sends, odd_sends, after=()):
    shape = (even_sends.shape, even_sends.dtype)
    (sent,) = call(pick_kernel, [shape], [even_sends, odd_sends], HINT["pick"], (), after)
    return sent


def picked_far(even_sends, odd_sends):
    shape = (even_sends.shape, even_sends.dtype)
    sem = [pltpu.SemaphoreType.DMA]
    (sent,) = call(pick_far_kernel, [shape], [odd_sends], HINT["pick"], sem, [even_sends])
    return sent


def exchanged(even_sends, odd_sends, after=()):
    return swapped(picked(even_sends, odd_sends, after), "ctx", 1)


def earlier_blocks(block, most):
    blocks = {0: block}
    for distance in range(2, most + 1, 2):
        blocks[distance] = shifted(blocks[distance - 2], 2)
        sent = picked_far(blocks[distance - 2], blocks[distance])
        blocks[distance - 1] = swapped(sent, "ctx", 1)
    return blocks


def local(queries, keys, values, gates, out_weight, grad_out, lengths):
    q, k, v, gate_rows, out_grad = queries[0], keys[0], values[0], gates[0], grad_out[0]
    tok, width = q.shape
    model = out_grad.shape[1]
    count, cores = lax.axis_size("ctx"), lax.axis_size("dp")
    reach = min(8, count // 2)
    mid = reach // 2
    one, wide = [((tok, width), BF16)], [((tok, width), F32)]
    total = pltpu.VMEM((tok, width), F32)
    key_at = earlier_blocks(k, mid)
    value_at = earlier_blocks(v, mid)
    query_at = {0: q}
    for distance in range(2, reach + 1, 2):
        query_at[distance] = shifted(query_at[distance - 2], -2)

    near = list(range(mid + 1))
    back = list(range(1, mid + 1))
    far = [mid + d for d in back]
    back_keys = [key_at[d] for d in back] + [value_at[d] for d in back]
    near_keys = [key_at[d] for d in near] + [value_at[d] for d in near]
    (far_attend,) = call(
        functools.partial(attend_kernel, mid, far),
        [((len(far) * width // HEAD, tok, tok), BF16)],
        [lengths, query_at[mid], *[key_at[d] for d in back]],
        HINT["attend"],
    )
    (far_term,) = call(
        functools.partial(far_kernel, mid, far),
        one,
        [lengths, far_attend, *[value_at[d] for d in back]],
        HINT["far_mix"],
        [total],
    )
    far_mixed = shifted(far_term, mid)
    for distance in range(1, reach, 2):
        query_at[distance] = exchanged(query_at[distance + 1], query_at[distance - 1], [far_term])
    grad_gated, near_mixed = call(
        functools.partial(mix_kernel, near),
        wide * 2,
        [lengths, q, *near_keys, out_grad, out_weight],
        HINT["near_mix"],
        (),
        [query_at[reach]],
    )
    gated, normed, grad_mixed = call(
        norm_kernel,
        [*one, *wide, *one],
        [near_mixed, far_mixed, grad_gated, gate_rows],
        HINT["norm"],
    )
    chunk = (width // (count * cores), model)
    keep, give = call(
        weight_kernel,
        [((count, *chunk), F32), ((count, *chunk), BF16)],
        [gated, out_grad],
        HINT["weight"],
        [pltpu.VMEM((width, model), F32)],
        [query_at[1]],
    )
    came = swapped(give, "dp", 1)
    step, parts = 1, count
    while parts > 4:
        parts //= 2
        keep, give = call(
            functools.partial(part_kernel, step),
            [((parts, *chunk), F32), ((parts, *chunk), BF16)],
            [keep, came],
            HINT["part"],
        )
        came = swapped(give, "ctx", step)
        step *= 2
    (near_query,) = call(
        functools.partial(query_grad_kernel, 0, near),
        wide,
        [lengths, q, grad_mixed, *near_keys],
        HINT["near_query"],
        [total],
        [keep],
    )
    output, grad_gates = call(
        out_kernel,
        [((tok, model), BF16), *one],
        [gated, out_weight, grad_gated, normed],
        HINT["out"],
        (),
        [keep],
    )
    grad_at = {0: grad_mixed, 2: shifted(grad_mixed, -2)}
    grad_at[2], *_ = lax.optimization_barrier([grad_at[2], near_query, output])
    for distance in range(4, reach + 1, 2):
        grad_at[distance] = shifted(grad_at[distance - 2], -2)
    (far_query_term,) = call(
        functools.partial(query_grad_kernel, mid, far),
        one,
        [lengths, query_at[mid], grad_at[mid], *back_keys],
        HINT["far_query"],
        [total],
    )
    far_query = shifted(far_query_term, mid)
    sent = {1: picked(grad_at[2], grad_mixed, [far_query_term])}
    groups = [[d for d in part if d % 2 == odd] for part in (near, far) for odd in (0, 1)]

    def key_terms(n, carried, after=()):
        group, last = groups[n], n == len(groups) - 1
        return call(
            functools.partial(key_grad_kernel, group, last),
            one * 3 if last else wide * 2,
            [lengths, k, v, *[query_at[d] for d in group], *[grad_at[d] for d in group], *carried],
            HINT["keys"][n],
            [total] * 2 if last else (),
            after,
        )

    for distance in range(3, reach, 2):
        sent[distance] = picked(grad_at[distance + 1], grad_at[distance - 1])
    for distance, block in sent.items():
        grad_at[distance] = swapped(block, "ctx", 1)
    grads = key_terms(0, [], [query_at[reach - 1]])
    grads = key_terms(1, grads, [far_query])
    keep, *gives = call(
        functools.partial(spread_kernel, step),
        [((1, *chunk), F32)] + [((1, *chunk), BF16)] * (parts - 1),
        [keep, came],
        HINT["part"],
        (),
        [sent[1]],
    )
    shares = [swapped(give, "ctx", (n + 1) * step) for n, give in enumerate(gives)]
    grad_weight, summed = call(
        functools.partial(sum_kernel, 1.0 / math.sqrt(cores * count * tok)),
        [(chunk, F32), ((8, HEAD), F32)],
        [keep, *shares],
        HINT["sum"],
    )
    grads = key_terms(2, grads, [summed])
    key_grad, value_grad, query_grad = key_terms(3, [*grads, near_query, far_query])
    return (
        output[None],
        grad_weight,
        query_grad[None],
        key_grad[None],
        value_grad[None],
        grad_gates[None],
    )


def solution(mesh):
    rows = P(("groups", "dp"), "ctx", None)
    in_specs = (rows, rows, rows, rows, P(), rows, P(("groups", "dp"), None))
    out_specs = (rows, P(("groups", "ctx", "dp"), None), rows, rows, rows, rows)
    return jax.shard_map(local, mesh=mesh, in_specs=in_specs, out_specs=out_specs, check_vma=False)
```

```python
import functools
import math

import jax
import jax.numpy as jnp
from jax import lax
from jax.experimental import pallas as pl
from jax.experimental.pallas import tpu as pltpu
from jax.sharding import PartitionSpec as P

HEAD = 128
EPS = 1e-05
SCALE = 1.0 / math.sqrt(HEAD)
BF16 = jnp.bfloat16
F32 = jnp.float32
VMEM = pl.BlockSpec(memory_space=pltpu.VMEM)
HINT = {
    "pick": 10.0,
    "attend": 0.001,
    "far_mix": 0.001,
    "near_mix": 0.001,
    "norm": 0.001,
    "near_query": 0.001,
    "weight": 0.001,
    "out": 0.001,
    "part": 0.001,
    "sum": 0.001,
    "far_query": 0.001,
    "keys": (0.001, 0.001, 0.001, 4.0, 0.001),
}
ANY = pl.BlockSpec(memory_space=pl.ANY)


def shifted(block, distance):
    devices = range(lax.axis_size("ctx"))
    return lax.ppermute(block, "ctx", [(i, i + distance) for i in devices if i + distance in devices])


def swapped(block, axis, step):
    return lax.ppermute(block, axis, [(i, i ^ step) for i in range(lax.axis_size(axis))])


def dot(a, b, da, db):
    return lax.dot_general(a, b, (((da,), (db,)), ((), ())), preferred_element_type=F32)


def ends_of(lengths_ref):
    ends, total = [], jnp.int32(0)
    for user in range(lengths_ref.shape[1]):
        total = total + lengths_ref[0, user]
        ends.append(total)
    return ends


def first_place(ends, places):
    first = jnp.zeros_like(places)
    for end in ends:
        first = jnp.where(places >= end, end, first)
    return first


def past_place(ends, places):
    past = jnp.zeros_like(places) + ends[-1]
    for end in ends[-2::-1]:
        past = jnp.where(places < end, end, past)
    return past


def crossing(ends, place, distance, tok):
    return first_place(ends, place) - (place - distance * tok), past_place(ends, place) - place


def own_mask(ends, place, tok, transposed):
    rows = place + lax.broadcasted_iota(jnp.int32, (tok, tok), 0)
    columns = place + lax.broadcasted_iota(jnp.int32, (tok, tok), 1)
    ids = place + lax.broadcasted_iota(jnp.int32, (tok, 1), 0)
    if transposed:
        return (columns >= rows) & (columns < past_place(ends, ids))
    return (columns <= rows) & (columns >= first_place(ends, ids))


def row_numbers(tok):
    return lax.broadcasted_iota(jnp.int32, (tok, HEAD), 0)


def half_scores(a, b):
    return dot(a, b, 1, 1) * (0.5 * SCALE)


def silu(half):
    return half * jnp.tanh(half) + half


def slopes(half):
    turn = jnp.tanh(half)
    attend = half * turn + half
    return attend, (1.0 + turn) + attend * (1.0 - turn)


def staggered(width, begin, finish):
    heads = [slice(h, h + HEAD) for h in range(0, width, HEAD)]
    begun = begin(heads[0])
    for now, after in zip(heads, heads[1:] + [None]):
        ready = begun
        if after is not None:
            begun = begin(after)
        finish(now, ready)


def mix_kernel(distances, *refs):
    count = len(distances)
    lengths_ref, q_ref = refs[:2]
    k_refs, v_refs = refs[2 : 2 + count], refs[2 + count : 2 + 2 * count]
    out_grad_ref, weight_ref, grad_gated_ref, total_ref = refs[2 + 2 * count :]
    grad_gated_ref[...] = dot(out_grad_ref[...], weight_ref[...], 1, 1)
    tok, width = q_ref.shape
    place = lax.axis_index("ctx") * tok
    ends = ends_of(lengths_ref)

    def pair(k_ref, v_ref, mask, dead, alive):
        def finish(cols, half):
            attend = silu(half)
            if mask is not None:
                total_ref[:, cols] = dot(jnp.where(mask, attend, 0.0).astype(BF16), v_ref[:, cols], 1, 0)
                return
            number = row_numbers(tok)
            v = jnp.where(number >= dead, v_ref[:, cols], 0.0).astype(BF16)
            term = dot(attend.astype(BF16), v, 1, 0)
            total_ref[:, cols] += jnp.where(number < alive, term, 0.0)

        staggered(width, lambda cols: half_scores(q_ref[:, cols], k_ref[:, cols]), finish)

    for n, distance in enumerate(distances):
        if distance == 0:
            pair(k_refs[n], v_refs[n], own_mask(ends, place, tok, False), None, None)
        else:
            dead, alive = crossing(ends, place, distance, tok)
            pl.when(dead < tok)(functools.partial(pair, k_refs[n], v_refs[n], None, dead, alive))


def attend_kernel(ahead, distances, *refs):
    lengths_ref, q_ref = refs[:2]
    attend_ref = refs[-1]
    tok, width = q_ref.shape
    heads = width // HEAD
    place = (lax.axis_index("ctx") + ahead) * tok
    ends = ends_of(lengths_ref)
    for n, distance in enumerate(distances):
        dead, alive = crossing(ends, place, distance, tok)

        @pl.when(dead < tok)
        def _(n=n, dead=dead, alive=alive):
            number = row_numbers(tok)

            def begin(cols):
                q = jnp.where(number < alive, q_ref[:, cols], 0.0).astype(BF16)
                return half_scores(q, jnp.where(number >= dead, refs[2 + n][:, cols], 0.0).astype(BF16))

            def finish(cols, half):
                attend_ref[n * heads + cols.start // HEAD] = silu(half).astype(BF16)

            staggered(width, begin, finish)


def far_kernel(ahead, distances, *refs):
    lengths_ref, attend_ref = refs[:2]
    mixed_ref, total_ref = refs[-2:]
    tok, width = mixed_ref.shape
    heads = width // HEAD
    place = (lax.axis_index("ctx") + ahead) * tok
    ends = ends_of(lengths_ref)
    total_ref[...] = jnp.zeros_like(total_ref)
    for n, distance in enumerate(distances):
        dead, _ = crossing(ends, place, distance, tok)

        @pl.when(dead < tok)
        def _(n=n):
            for head in range(heads):
                cols = slice(head * HEAD, (head + 1) * HEAD)
                total_ref[:, cols] += dot(attend_ref[n * heads + head], refs[2 + n][:, cols], 1, 0)

    mixed_ref[...] = total_ref[...].astype(BF16)


def norm_kernel(near_ref, far_ref, grad_gated_ref, gates_ref, gated_ref, normed_ref, grad_mixed_ref):
    mixed = near_ref[...] + far_ref[...].astype(F32)
    gates = gates_ref[...].astype(F32)
    grad_gated = grad_gated_ref[...]
    centered = mixed - jnp.mean(mixed, axis=1, keepdims=True)
    inverse = lax.rsqrt(jnp.mean(centered * centered, axis=1, keepdims=True) + EPS)
    normed = centered * inverse
    gated_ref[...] = (normed * gates).astype(BF16)
    normed_ref[...] = normed
    grad_normed = grad_gated * gates
    grad_mixed_ref[...] = (
        (
            grad_normed
            - jnp.mean(grad_normed, axis=1, keepdims=True)
            - normed * jnp.mean(grad_normed * normed, axis=1, keepdims=True)
        )
        * inverse
    ).astype(BF16)


def query_grad_kernel(ahead, distances, *refs):
    count = len(distances)
    lengths_ref, q_ref, grad_ref = refs[:3]
    k_refs, v_refs = refs[3 : 3 + count], refs[3 + count : 3 + 2 * count]
    out_ref, total_ref = refs[-2:]
    tok, width = q_ref.shape
    place = (lax.axis_index("ctx") + ahead) * tok
    ends = ends_of(lengths_ref)

    def pair(k_ref, v_ref, mask, dead, alive):
        def begin(cols):
            return half_scores(q_ref[:, cols], k_ref[:, cols]), dot(grad_ref[:, cols], v_ref[:, cols], 1, 1)

        def finish(cols, begun):
            half, pull = begun
            score_grad = pull * slopes(half)[1]
            if mask is not None:
                total_ref[:, cols] = dot(jnp.where(mask, score_grad, 0.0).astype(BF16), k_ref[:, cols], 1, 0)
                return
            number = row_numbers(tok)
            k = jnp.where(number >= dead, k_ref[:, cols], 0.0).astype(BF16)
            term = dot(score_grad.astype(BF16), k, 1, 0)
            total_ref[:, cols] += jnp.where(number < alive, term, 0.0)

        staggered(width, begin, finish)

    if distances[0] > 0:
        total_ref[...] = jnp.zeros_like(total_ref)
    for n, distance in enumerate(distances):
        if distance == 0:
            pair(k_refs[n], v_refs[n], own_mask(ends, place, tok, False), None, None)
        else:
            dead, alive = crossing(ends, place, distance, tok)
            pl.when(dead < tok)(functools.partial(pair, k_refs[n], v_refs[n], None, dead, alive))
    total = total_ref[...] * (0.5 * SCALE)
    out_ref[...] = total.astype(out_ref.dtype)


def key_grad_kernel(distances, last, *refs):
    count = len(distances)
    lengths_ref, k_ref, v_ref = refs[:3]
    q_refs, grad_refs = refs[3 : 3 + count], refs[3 + count : 3 + 2 * count]
    if last:
        near_ref, far_ref, key_out, value_out, query_out, key_total, value_total = refs[-7:]
        query_out[...] = (near_ref[...] + far_ref[...].astype(F32)).astype(BF16)
    else:
        key_total, value_total = refs[-2:]
    tok, width = k_ref.shape
    place = lax.axis_index("ctx") * tok
    ends = ends_of(lengths_ref)

    def pair(q_ref, grad_ref, mask, dead, alive):
        def begin(cols):
            return half_scores(k_ref[:, cols], q_ref[:, cols]), dot(v_ref[:, cols], grad_ref[:, cols], 1, 1)

        def finish(cols, begun):
            half, pull = begun
            attend, slope = slopes(half)
            score_grad = pull * slope
            if mask is not None:
                value_total[:, cols] = dot(jnp.where(mask, attend, 0.0).astype(BF16), grad_ref[:, cols], 1, 0)
                key_total[:, cols] = dot(jnp.where(mask, score_grad, 0.0).astype(BF16), q_ref[:, cols], 1, 0)
                return
            number = row_numbers(tok)
            grad = jnp.where(number < alive, grad_ref[:, cols], 0.0).astype(BF16)
            q = jnp.where(number < alive, q_ref[:, cols], 0.0).astype(BF16)
            value_term = dot(attend.astype(BF16), grad, 1, 0)
            key_term = dot(score_grad.astype(BF16), q, 1, 0)
            value_total[:, cols] += jnp.where(number >= dead, value_term, 0.0)
            key_total[:, cols] += jnp.where(number >= dead, key_term, 0.0)

        staggered(width, begin, finish)

    if distances[0] > 0:
        key_total[...] = refs[3 + 2 * count][...]
        value_total[...] = refs[4 + 2 * count][...]
    for n, distance in enumerate(distances):
        if distance == 0:
            pair(q_refs[n], grad_refs[n], own_mask(ends, place, tok, True), None, None)
        else:
            dead, alive = crossing(ends, place + distance * tok, distance, tok)
            pl.when(dead < tok)(functools.partial(pair, q_refs[n], grad_refs[n], None, dead, alive))
    if last:
        key_out[...] = (key_total[...] * (0.5 * SCALE)).astype(BF16)
        value_out[...] = value_total[...].astype(BF16)


def parted(total, bit, keep_ref, give_ref):
    for part in range(keep_ref.shape[0]):
        keep_ref[part] = total(2 * part + bit)
        give_ref[part] = total(2 * part + 1 - bit).astype(BF16)


def out_kernel(gated_ref, weight_ref, grad_gated_ref, normed_ref, out_ref, grad_gates_ref):
    grad_gates_ref[...] = (grad_gated_ref[...] * normed_ref[...]).astype(BF16)
    out_ref[...] = dot(gated_ref[...], weight_ref[...], 1, 0).astype(BF16)


def weight_kernel(gated_ref, out_grad_ref, keep_ref, give_ref, total_ref):
    total_ref[...] = dot(gated_ref[...], out_grad_ref[...], 0, 0)
    rows = keep_ref.shape[1]
    parted(
        lambda chunk: total_ref[pl.ds(pl.multiple_of(chunk * rows, rows), rows), :],
        lax.axis_index("dp"),
        keep_ref,
        give_ref,
    )


def part_kernel(step, kept_ref, came_ref, keep_ref, give_ref):
    parted(
        lambda chunk: kept_ref[chunk] + came_ref[chunk].astype(F32),
        (lax.axis_index("ctx") // step) % 2,
        keep_ref,
        give_ref,
    )


def spread_kernel(step, kept_ref, came_ref, keep_ref, *give_refs):
    own = lax.axis_index("ctx") // step
    keep_ref[0] = kept_ref[own] + came_ref[own].astype(F32)
    for n, give_ref in enumerate(give_refs):
        chunk = own ^ (n + 1)
        give_ref[0] = (kept_ref[chunk] + came_ref[chunk].astype(F32)).astype(BF16)


def sum_kernel(factor, kept_ref, *refs):
    rows = kept_ref[0]
    for came_ref in refs[:-2]:
        rows = rows + came_ref[0].astype(F32)
    out_ref, mark_ref = refs[-2:]
    out_ref[...] = rows * factor
    mark_ref[...] = jnp.zeros_like(mark_ref)


def pick_kernel(even_ref, odd_ref, out_ref):
    even = lax.axis_index("ctx") % 2 == 0

    @pl.when(even)
    def _():
        out_ref[...] = even_ref[...]

    @pl.when(jnp.logical_not(even))
    def _():
        out_ref[...] = odd_ref[...]


def pick_far_kernel(odd_ref, even_ref, out_ref, sem):
    even = lax.axis_index("ctx") % 2 == 0

    @pl.when(even)
    def _():
        copy = pltpu.make_async_copy(even_ref, out_ref, sem)
        copy.start()
        copy.wait()

    @pl.when(jnp.logical_not(even))
    def _():
        out_ref[...] = odd_ref[...]


def call(kernel, outs, args, micros, scratch=(), after=()):
    held = len(args)

    def body(*refs):
        kernel(*refs[:held], *refs[held + len(after) :])

    if kernel is pick_far_kernel:
        body = kernel

    shapes = [jax.ShapeDtypeStruct(shape, dtype) for shape, dtype in outs]
    return pl.pallas_call(
        body,
        out_shape=shapes,
        in_specs=[VMEM] * len(args) + [ANY] * len(after),
        out_specs=[VMEM] * len(shapes),
        scratch_shapes=list(scratch),
        cost_estimate=pl.CostEstimate(flops=int(micros * 1.1535e9), bytes_accessed=0, transcendentals=0),
        compiler_params=pltpu.CompilerParams(vmem_limit_bytes=48 * 1024 * 1024),
    )(*args, *after)


def picked(even_sends, odd_sends, after=()):
    shape = (even_sends.shape, even_sends.dtype)
    (sent,) = call(pick_kernel, [shape], [even_sends, odd_sends], HINT["pick"], (), after)
    return sent


def picked_far(even_sends, odd_sends):
    shape = (even_sends.shape, even_sends.dtype)
    sem = [pltpu.SemaphoreType.DMA]
    (sent,) = call(pick_far_kernel, [shape], [odd_sends], HINT["pick"], sem, [even_sends])
    return sent


def exchanged(even_sends, odd_sends, after=()):
    return swapped(picked(even_sends, odd_sends, after), "ctx", 1)


def earlier_blocks(block, most):
    blocks = {0: block}
    for distance in range(2, most + 1, 2):
        blocks[distance] = shifted(blocks[distance - 2], 2)
        sent = picked_far(blocks[distance - 2], blocks[distance])
        blocks[distance - 1] = swapped(sent, "ctx", 1)
    return blocks


def local(queries, keys, values, gates, out_weight, grad_out, lengths):
    q, k, v, gate_rows, out_grad = queries[0], keys[0], values[0], gates[0], grad_out[0]
    tok, width = q.shape
    model = out_grad.shape[1]
    count, cores = lax.axis_size("ctx"), lax.axis_size("dp")
    reach = min(8, count // 2)
    mid = reach // 2
    one, wide = [((tok, width), BF16)], [((tok, width), F32)]
    total = pltpu.VMEM((tok, width), F32)
    key_at = earlier_blocks(k, mid)
    value_at = earlier_blocks(v, mid)
    query_at = {0: q}
    for distance in range(2, reach + 1, 2):
        query_at[distance] = shifted(query_at[distance - 2], -2)

    near = list(range(mid + 1))
    back = list(range(1, mid + 1))
    far = [mid + d for d in back]
    back_keys = [key_at[d] for d in back] + [value_at[d] for d in back]
    near_keys = [key_at[d] for d in near] + [value_at[d] for d in near]
    (far_attend,) = call(
        functools.partial(attend_kernel, mid, far),
        [((len(far) * width // HEAD, tok, tok), BF16)],
        [lengths, query_at[mid], *[key_at[d] for d in back]],
        HINT["attend"],
    )
    (far_term,) = call(
        functools.partial(far_kernel, mid, far),
        one,
        [lengths, far_attend, *[value_at[d] for d in back]],
        HINT["far_mix"],
        [total],
    )
    far_mixed = shifted(far_term, mid)
    for distance in range(1, reach, 2):
        query_at[distance] = exchanged(query_at[distance + 1], query_at[distance - 1], [far_term])
    grad_gated, near_mixed = call(
        functools.partial(mix_kernel, near),
        wide * 2,
        [lengths, q, *near_keys, out_grad, out_weight],
        HINT["near_mix"],
        (),
        [query_at[reach]],
    )
    gated, normed, grad_mixed = call(
        norm_kernel,
        [*one, *wide, *one],
        [near_mixed, far_mixed, grad_gated, gate_rows],
        HINT["norm"],
    )
    chunk = (width // (count * cores), model)
    (near_query,) = call(
        functools.partial(query_grad_kernel, 0, near),
        wide,
        [lengths, q, grad_mixed, *near_keys],
        HINT["near_query"],
        [total],
    )
    keep, give = call(
        weight_kernel,
        [((count, *chunk), F32), ((count, *chunk), BF16)],
        [gated, out_grad],
        HINT["weight"],
        [pltpu.VMEM((width, model), F32)],
        [near_query, query_at[1]],
    )
    came = swapped(give, "dp", 1)
    step, parts = 1, count
    while parts > 4:
        parts //= 2
        keep, give = call(
            functools.partial(part_kernel, step),
            [((parts, *chunk), F32), ((parts, *chunk), BF16)],
            [keep, came],
            HINT["part"],
        )
        came = swapped(give, "ctx", step)
        step *= 2
    output, grad_gates = call(
        out_kernel,
        [((tok, model), BF16), *one],
        [gated, out_weight, grad_gated, normed],
        HINT["out"],
        (),
        [keep],
    )
    grad_at = {0: grad_mixed}

    groups = [[0]] + [[d for d in part if d > 0 and d % 2 == odd] for part in (near, far) for odd in (0, 1)]

    def key_terms(n, carried, after=()):
        group, last = groups[n], n == len(groups) - 1
        return call(
            functools.partial(key_grad_kernel, group, last),
            one * 3 if last else wide * 2,
            [lengths, k, v, *[query_at[d] for d in group], *[grad_at[d] for d in group], *carried],
            HINT["keys"][n],
            [total] * 2 if last else (),
            after,
        )

    grads = key_terms(0, [], [keep])
    grad_at[2], *_ = lax.optimization_barrier([shifted(grad_mixed, -2), near_query, output, *grads])
    for distance in range(4, reach + 1, 2):
        grad_at[distance] = shifted(grad_at[distance - 2], -2)
    (far_query_term,) = call(
        functools.partial(query_grad_kernel, mid, far),
        one,
        [lengths, query_at[mid], grad_at[mid], *back_keys],
        HINT["far_query"],
        [total],
    )
    far_query = shifted(far_query_term, mid)
    sent = {1: picked(grad_at[2], grad_mixed, [far_query_term])}
    for distance in range(3, reach, 2):
        sent[distance] = picked(grad_at[distance + 1], grad_at[distance - 1])
    for distance, block in sent.items():
        grad_at[distance] = swapped(block, "ctx", 1)
    grads = key_terms(1, grads, [query_at[reach - 1]])
    grads = key_terms(2, grads)
    keep, *gives = call(
        functools.partial(spread_kernel, step),
        [((1, *chunk), F32)] + [((1, *chunk), BF16)] * (parts - 1),
        [keep, came],
        HINT["part"],
        (),
        [sent[1]],
    )
    shares = [swapped(give, "ctx", (n + 1) * step) for n, give in enumerate(gives)]
    grad_weight, summed = call(
        functools.partial(sum_kernel, 1.0 / math.sqrt(cores * count * tok)),
        [(chunk, F32), ((8, HEAD), F32)],
        [keep, *shares],
        HINT["sum"],
    )
    grads = key_terms(3, grads, [summed, far_query])
    key_grad, value_grad, query_grad = key_terms(4, [*grads, near_query, far_query])
    return (
        output[None],
        grad_weight,
        query_grad[None],
        key_grad[None],
        value_grad[None],
        grad_gates[None],
    )


def solution(mesh):
    rows = P(("groups", "dp"), "ctx", None)
    in_specs = (rows, rows, rows, rows, P(), rows, P(("groups", "dp"), None))
    out_specs = (rows, P(("groups", "ctx", "dp"), None), rows, rows, rows, rows)
    return jax.shard_map(local, mesh=mesh, in_specs=in_specs, out_specs=out_specs, check_vma=False)
```

```python
import functools
import math

import jax
import jax.numpy as jnp
from jax import lax
from jax.experimental import pallas as pl
from jax.experimental.pallas import tpu as pltpu
from jax.sharding import PartitionSpec as P

HEAD = 128
EPS = 1e-05
SCALE = 1.0 / math.sqrt(HEAD)
BF16 = jnp.bfloat16
F32 = jnp.float32
VMEM = pl.BlockSpec(memory_space=pltpu.VMEM)
HINT = {
    "pick": 10.0,
    "attend": 0.001,
    "far_mix": 0.001,
    "near_mix": 0.001,
    "norm": 0.001,
    "near_query": 0.001,
    "weight": 0.001,
    "out": 0.001,
    "part": 0.001,
    "sum": 0.001,
    "far_query": 0.001,
    "keys": (0.001, 0.001, 0.001, 4.0, 0.001),
}
ANY = pl.BlockSpec(memory_space=pl.ANY)


def shifted(block, distance):
    devices = range(lax.axis_size("ctx"))
    return lax.ppermute(block, "ctx", [(i, i + distance) for i in devices if i + distance in devices])


def swapped(block, axis, step):
    return lax.ppermute(block, axis, [(i, i ^ step) for i in range(lax.axis_size(axis))])


def dot(a, b, da, db):
    return lax.dot_general(a, b, (((da,), (db,)), ((), ())), preferred_element_type=F32)


def ends_of(lengths_ref):
    ends, total = [], jnp.int32(0)
    for user in range(lengths_ref.shape[1]):
        total = total + lengths_ref[0, user]
        ends.append(total)
    return ends


def first_place(ends, places):
    first = jnp.zeros_like(places)
    for end in ends:
        first = jnp.where(places >= end, end, first)
    return first


def past_place(ends, places):
    past = jnp.zeros_like(places) + ends[-1]
    for end in ends[-2::-1]:
        past = jnp.where(places < end, end, past)
    return past


def crossing(ends, place, distance, tok):
    return first_place(ends, place) - (place - distance * tok), past_place(ends, place) - place


def own_mask(ends, place, tok, transposed):
    rows = place + lax.broadcasted_iota(jnp.int32, (tok, tok), 0)
    columns = place + lax.broadcasted_iota(jnp.int32, (tok, tok), 1)
    ids = place + lax.broadcasted_iota(jnp.int32, (tok, 1), 0)
    if transposed:
        return (columns >= rows) & (columns < past_place(ends, ids))
    return (columns <= rows) & (columns >= first_place(ends, ids))


def row_numbers(tok):
    return lax.broadcasted_iota(jnp.int32, (tok, HEAD), 0)


def half_scores(a, b):
    return dot(a, b, 1, 1) * (0.5 * SCALE)


def silu(half):
    return half * jnp.tanh(half) + half


def slopes(half):
    turn = jnp.tanh(half)
    attend = half * turn + half
    return attend, (1.0 + turn) + attend * (1.0 - turn)


def staggered(width, begin, finish):
    heads = [slice(h, h + HEAD) for h in range(0, width, HEAD)]
    begun = begin(heads[0])
    for now, after in zip(heads, heads[1:] + [None]):
        ready = begun
        if after is not None:
            begun = begin(after)
        finish(now, ready)


def mix_kernel(distances, *refs):
    count = len(distances)
    lengths_ref, q_ref = refs[:2]
    k_refs, v_refs = refs[2 : 2 + count], refs[2 + count : 2 + 2 * count]
    out_grad_ref, weight_ref, grad_gated_ref, total_ref = refs[2 + 2 * count :]
    grad_gated_ref[...] = dot(out_grad_ref[...], weight_ref[...], 1, 1)
    tok, width = q_ref.shape
    place = lax.axis_index("ctx") * tok
    ends = ends_of(lengths_ref)

    def pair(k_ref, v_ref, mask, dead, alive):
        def finish(cols, half):
            attend = silu(half)
            if mask is not None:
                total_ref[:, cols] = dot(jnp.where(mask, attend, 0.0).astype(BF16), v_ref[:, cols], 1, 0)
                return
            number = row_numbers(tok)
            v = jnp.where(number >= dead, v_ref[:, cols], 0.0).astype(BF16)
            term = dot(attend.astype(BF16), v, 1, 0)
            total_ref[:, cols] += jnp.where(number < alive, term, 0.0)

        staggered(width, lambda cols: half_scores(q_ref[:, cols], k_ref[:, cols]), finish)

    for n, distance in enumerate(distances):
        if distance == 0:
            pair(k_refs[n], v_refs[n], own_mask(ends, place, tok, False), None, None)
        else:
            dead, alive = crossing(ends, place, distance, tok)
            pl.when(dead < tok)(functools.partial(pair, k_refs[n], v_refs[n], None, dead, alive))


def attend_kernel(ahead, distances, *refs):
    lengths_ref, q_ref = refs[:2]
    attend_ref = refs[-1]
    tok, width = q_ref.shape
    heads = width // HEAD
    place = (lax.axis_index("ctx") + ahead) * tok
    ends = ends_of(lengths_ref)
    for n, distance in enumerate(distances):
        dead, alive = crossing(ends, place, distance, tok)

        @pl.when(dead < tok)
        def _(n=n, dead=dead, alive=alive):
            number = row_numbers(tok)

            def begin(cols):
                q = jnp.where(number < alive, q_ref[:, cols], 0.0).astype(BF16)
                return half_scores(q, jnp.where(number >= dead, refs[2 + n][:, cols], 0.0).astype(BF16))

            def finish(cols, half):
                attend_ref[n * heads + cols.start // HEAD] = silu(half).astype(BF16)

            staggered(width, begin, finish)


def far_kernel(ahead, distances, *refs):
    lengths_ref, attend_ref = refs[:2]
    mixed_ref, total_ref = refs[-2:]
    tok, width = mixed_ref.shape
    heads = width // HEAD
    place = (lax.axis_index("ctx") + ahead) * tok
    ends = ends_of(lengths_ref)
    total_ref[...] = jnp.zeros_like(total_ref)
    for n, distance in enumerate(distances):
        dead, _ = crossing(ends, place, distance, tok)

        @pl.when(dead < tok)
        def _(n=n):
            for head in range(heads):
                cols = slice(head * HEAD, (head + 1) * HEAD)
                total_ref[:, cols] += dot(attend_ref[n * heads + head], refs[2 + n][:, cols], 1, 0)

    mixed_ref[...] = total_ref[...].astype(BF16)


def norm_kernel(near_ref, far_ref, grad_gated_ref, gates_ref, gated_ref, normed_ref, grad_mixed_ref):
    mixed = near_ref[...] + far_ref[...].astype(F32)
    gates = gates_ref[...].astype(F32)
    grad_gated = grad_gated_ref[...]
    centered = mixed - jnp.mean(mixed, axis=1, keepdims=True)
    inverse = lax.rsqrt(jnp.mean(centered * centered, axis=1, keepdims=True) + EPS)
    normed = centered * inverse
    gated_ref[...] = (normed * gates).astype(BF16)
    normed_ref[...] = normed
    grad_normed = grad_gated * gates
    grad_mixed_ref[...] = (
        (
            grad_normed
            - jnp.mean(grad_normed, axis=1, keepdims=True)
            - normed * jnp.mean(grad_normed * normed, axis=1, keepdims=True)
        )
        * inverse
    ).astype(BF16)


def query_grad_kernel(ahead, distances, *refs):
    count = len(distances)
    lengths_ref, q_ref, grad_ref = refs[:3]
    k_refs, v_refs = refs[3 : 3 + count], refs[3 + count : 3 + 2 * count]
    out_ref, total_ref = refs[-2:]
    tok, width = q_ref.shape
    place = (lax.axis_index("ctx") + ahead) * tok
    ends = ends_of(lengths_ref)

    def pair(k_ref, v_ref, mask, dead, alive):
        def begin(cols):
            return half_scores(q_ref[:, cols], k_ref[:, cols]), dot(grad_ref[:, cols], v_ref[:, cols], 1, 1)

        def finish(cols, begun):
            half, pull = begun
            score_grad = pull * slopes(half)[1]
            if mask is not None:
                total_ref[:, cols] = dot(jnp.where(mask, score_grad, 0.0).astype(BF16), k_ref[:, cols], 1, 0)
                return
            number = row_numbers(tok)
            k = jnp.where(number >= dead, k_ref[:, cols], 0.0).astype(BF16)
            term = dot(score_grad.astype(BF16), k, 1, 0)
            total_ref[:, cols] += jnp.where(number < alive, term, 0.0)

        staggered(width, begin, finish)

    def own(k_ref, v_ref, start, end):
        shape = (end - start, end)
        rows = place + start + lax.broadcasted_iota(jnp.int32, shape, 0)
        columns = place + lax.broadcasted_iota(jnp.int32, shape, 1)
        ids = place + start + lax.broadcasted_iota(jnp.int32, (end - start, 1), 0)
        live = (columns <= rows) & (columns >= first_place(ends, ids))

        def begin(cols):
            half = half_scores(q_ref[start:end, cols], k_ref[:end, cols])
            return half, dot(grad_ref[start:end, cols], v_ref[:end, cols], 1, 1)

        def finish(cols, begun):
            half, pull = begun
            score_grad = jnp.where(live, pull * slopes(half)[1], 0.0).astype(BF16)
            total_ref[start:end, cols] = dot(score_grad, k_ref[:end, cols], 1, 0)

        staggered(width, begin, finish)

    if distances[0] > 0:
        total_ref[...] = jnp.zeros_like(total_ref)
    for n, distance in enumerate(distances):
        if distance == 0:
            for start, end in ((0, tok // 2), (tok // 2, tok)):
                own(k_refs[n], v_refs[n], start, end)
        else:
            dead, alive = crossing(ends, place, distance, tok)
            pl.when(dead < tok)(functools.partial(pair, k_refs[n], v_refs[n], None, dead, alive))
    total = total_ref[...] * (0.5 * SCALE)
    out_ref[...] = total.astype(out_ref.dtype)


def key_grad_kernel(distances, last, *refs):
    count = len(distances)
    lengths_ref, k_ref, v_ref = refs[:3]
    q_refs, grad_refs = refs[3 : 3 + count], refs[3 + count : 3 + 2 * count]
    if last:
        near_ref, far_ref, key_out, value_out, query_out, key_total, value_total = refs[-7:]
        query_out[...] = (near_ref[...] + far_ref[...].astype(F32)).astype(BF16)
    else:
        key_total, value_total = refs[-2:]
    tok, width = k_ref.shape
    place = lax.axis_index("ctx") * tok
    ends = ends_of(lengths_ref)

    def pair(q_ref, grad_ref, mask, dead, alive):
        def begin(cols):
            return half_scores(k_ref[:, cols], q_ref[:, cols]), dot(v_ref[:, cols], grad_ref[:, cols], 1, 1)

        def finish(cols, begun):
            half, pull = begun
            attend, slope = slopes(half)
            score_grad = pull * slope
            if mask is not None:
                value_total[:, cols] = dot(jnp.where(mask, attend, 0.0).astype(BF16), grad_ref[:, cols], 1, 0)
                key_total[:, cols] = dot(jnp.where(mask, score_grad, 0.0).astype(BF16), q_ref[:, cols], 1, 0)
                return
            number = row_numbers(tok)
            grad = jnp.where(number < alive, grad_ref[:, cols], 0.0).astype(BF16)
            q = jnp.where(number < alive, q_ref[:, cols], 0.0).astype(BF16)
            value_term = dot(attend.astype(BF16), grad, 1, 0)
            key_term = dot(score_grad.astype(BF16), q, 1, 0)
            value_total[:, cols] += jnp.where(number >= dead, value_term, 0.0)
            key_total[:, cols] += jnp.where(number >= dead, key_term, 0.0)

        staggered(width, begin, finish)

    if distances[0] > 0:
        key_total[...] = refs[3 + 2 * count][...]
        value_total[...] = refs[4 + 2 * count][...]
    for n, distance in enumerate(distances):
        if distance == 0:
            pair(q_refs[n], grad_refs[n], own_mask(ends, place, tok, True), None, None)
        else:
            dead, alive = crossing(ends, place + distance * tok, distance, tok)
            pl.when(dead < tok)(functools.partial(pair, q_refs[n], grad_refs[n], None, dead, alive))
    if last:
        key_out[...] = (key_total[...] * (0.5 * SCALE)).astype(BF16)
        value_out[...] = value_total[...].astype(BF16)


def parted(total, bit, keep_ref, give_ref):
    for part in range(keep_ref.shape[0]):
        keep_ref[part] = total(2 * part + bit)
        give_ref[part] = total(2 * part + 1 - bit).astype(BF16)


def out_kernel(gated_ref, weight_ref, grad_gated_ref, normed_ref, out_ref, grad_gates_ref):
    grad_gates_ref[...] = (grad_gated_ref[...] * normed_ref[...]).astype(BF16)
    out_ref[...] = dot(gated_ref[...], weight_ref[...], 1, 0).astype(BF16)


def weight_kernel(gated_ref, out_grad_ref, keep_ref, give_ref, total_ref):
    total_ref[...] = dot(gated_ref[...], out_grad_ref[...], 0, 0)
    rows = keep_ref.shape[1]
    parted(
        lambda chunk: total_ref[pl.ds(pl.multiple_of(chunk * rows, rows), rows), :],
        lax.axis_index("dp"),
        keep_ref,
        give_ref,
    )


def part_kernel(step, kept_ref, came_ref, keep_ref, give_ref):
    parted(
        lambda chunk: kept_ref[chunk] + came_ref[chunk].astype(F32),
        (lax.axis_index("ctx") // step) % 2,
        keep_ref,
        give_ref,
    )


def spread_kernel(step, kept_ref, came_ref, keep_ref, *give_refs):
    own = lax.axis_index("ctx") // step
    keep_ref[0] = kept_ref[own] + came_ref[own].astype(F32)
    for n, give_ref in enumerate(give_refs):
        chunk = own ^ (n + 1)
        give_ref[0] = (kept_ref[chunk] + came_ref[chunk].astype(F32)).astype(BF16)


def sum_kernel(factor, kept_ref, *refs):
    rows = kept_ref[0]
    for came_ref in refs[:-2]:
        rows = rows + came_ref[0].astype(F32)
    out_ref, mark_ref = refs[-2:]
    out_ref[...] = rows * factor
    mark_ref[...] = jnp.zeros_like(mark_ref)


def pick_kernel(even_ref, odd_ref, out_ref):
    even = lax.axis_index("ctx") % 2 == 0

    @pl.when(even)
    def _():
        out_ref[...] = even_ref[...]

    @pl.when(jnp.logical_not(even))
    def _():
        out_ref[...] = odd_ref[...]


def pick_far_kernel(odd_ref, even_ref, out_ref, sem):
    even = lax.axis_index("ctx") % 2 == 0

    @pl.when(even)
    def _():
        copy = pltpu.make_async_copy(even_ref, out_ref, sem)
        copy.start()
        copy.wait()

    @pl.when(jnp.logical_not(even))
    def _():
        out_ref[...] = odd_ref[...]


def call(kernel, outs, args, micros, scratch=(), after=()):
    held = len(args)

    def body(*refs):
        kernel(*refs[:held], *refs[held + len(after) :])

    if kernel is pick_far_kernel:
        body = kernel

    shapes = [jax.ShapeDtypeStruct(shape, dtype) for shape, dtype in outs]
    return pl.pallas_call(
        body,
        out_shape=shapes,
        in_specs=[VMEM] * len(args) + [ANY] * len(after),
        out_specs=[VMEM] * len(shapes),
        scratch_shapes=list(scratch),
        cost_estimate=pl.CostEstimate(flops=int(micros * 1.1535e9), bytes_accessed=0, transcendentals=0),
        compiler_params=pltpu.CompilerParams(vmem_limit_bytes=48 * 1024 * 1024),
    )(*args, *after)


def picked(even_sends, odd_sends, after=()):
    shape = (even_sends.shape, even_sends.dtype)
    (sent,) = call(pick_kernel, [shape], [even_sends, odd_sends], HINT["pick"], (), after)
    return sent


def picked_far(even_sends, odd_sends):
    shape = (even_sends.shape, even_sends.dtype)
    sem = [pltpu.SemaphoreType.DMA]
    (sent,) = call(pick_far_kernel, [shape], [odd_sends], HINT["pick"], sem, [even_sends])
    return sent


def exchanged(even_sends, odd_sends, after=()):
    return swapped(picked(even_sends, odd_sends, after), "ctx", 1)


def earlier_blocks(block, most):
    blocks = {0: block}
    for distance in range(2, most + 1, 2):
        blocks[distance] = shifted(blocks[distance - 2], 2)
        sent = picked_far(blocks[distance - 2], blocks[distance])
        blocks[distance - 1] = swapped(sent, "ctx", 1)
    return blocks


def local(queries, keys, values, gates, out_weight, grad_out, lengths):
    q, k, v, gate_rows, out_grad = queries[0], keys[0], values[0], gates[0], grad_out[0]
    tok, width = q.shape
    model = out_grad.shape[1]
    count, cores = lax.axis_size("ctx"), lax.axis_size("dp")
    reach = min(8, count // 2)
    mid = reach // 2
    one, wide = [((tok, width), BF16)], [((tok, width), F32)]
    total = pltpu.VMEM((tok, width), F32)
    key_at = earlier_blocks(k, mid)
    value_at = earlier_blocks(v, mid)
    query_at = {0: q}
    for distance in range(2, reach + 1, 2):
        query_at[distance] = shifted(query_at[distance - 2], -2)

    near = list(range(mid + 1))
    back = list(range(1, mid + 1))
    far = [mid + d for d in back]
    back_keys = [key_at[d] for d in back] + [value_at[d] for d in back]
    near_keys = [key_at[d] for d in near] + [value_at[d] for d in near]
    (far_attend,) = call(
        functools.partial(attend_kernel, mid, far),
        [((len(far) * width // HEAD, tok, tok), BF16)],
        [lengths, query_at[mid], *[key_at[d] for d in back]],
        HINT["attend"],
    )
    (far_term,) = call(
        functools.partial(far_kernel, mid, far),
        one,
        [lengths, far_attend, *[value_at[d] for d in back]],
        HINT["far_mix"],
        [total],
    )
    far_mixed = shifted(far_term, mid)
    for distance in range(1, reach, 2):
        query_at[distance] = exchanged(query_at[distance + 1], query_at[distance - 1], [far_term])
    grad_gated, near_mixed = call(
        functools.partial(mix_kernel, near),
        wide * 2,
        [lengths, q, *near_keys, out_grad, out_weight],
        HINT["near_mix"],
        (),
        [query_at[reach]],
    )
    gated, normed, grad_mixed = call(
        norm_kernel,
        [*one, *wide, *one],
        [near_mixed, far_mixed, grad_gated, gate_rows],
        HINT["norm"],
    )
    chunk = (width // (count * cores), model)
    (near_query,) = call(
        functools.partial(query_grad_kernel, 0, near),
        wide,
        [lengths, q, grad_mixed, *near_keys],
        HINT["near_query"],
        [total],
    )
    keep, give = call(
        weight_kernel,
        [((count, *chunk), F32), ((count, *chunk), BF16)],
        [gated, out_grad],
        HINT["weight"],
        [pltpu.VMEM((width, model), F32)],
        [near_query, query_at[1]],
    )
    came = swapped(give, "dp", 1)
    step, parts = 1, count
    while parts > 4:
        parts //= 2
        keep, give = call(
            functools.partial(part_kernel, step),
            [((parts, *chunk), F32), ((parts, *chunk), BF16)],
            [keep, came],
            HINT["part"],
        )
        came = swapped(give, "ctx", step)
        step *= 2
    output, grad_gates = call(
        out_kernel,
        [((tok, model), BF16), *one],
        [gated, out_weight, grad_gated, normed],
        HINT["out"],
        (),
        [keep],
    )
    grad_at = {0: grad_mixed}

    groups = [[0]] + [[d for d in part if d > 0 and d % 2 == odd] for part in (near, far) for odd in (0, 1)]

    def key_terms(n, carried, after=()):
        group, last = groups[n], n == len(groups) - 1
        return call(
            functools.partial(key_grad_kernel, group, last),
            one * 3 if last else wide * 2,
            [lengths, k, v, *[query_at[d] for d in group], *[grad_at[d] for d in group], *carried],
            HINT["keys"][n],
            [total] * 2 if last else (),
            after,
        )

    grads = key_terms(0, [], [keep])
    grad_at[2], *_ = lax.optimization_barrier([shifted(grad_mixed, -2), near_query, output, *grads])
    for distance in range(4, reach + 1, 2):
        grad_at[distance] = shifted(grad_at[distance - 2], -2)
    (far_query_term,) = call(
        functools.partial(query_grad_kernel, mid, far),
        one,
        [lengths, query_at[mid], grad_at[mid], *back_keys],
        HINT["far_query"],
        [total],
    )
    far_query = shifted(far_query_term, mid)
    sent = {1: picked(grad_at[2], grad_mixed, [far_query_term])}
    for distance in range(3, reach, 2):
        sent[distance] = picked(grad_at[distance + 1], grad_at[distance - 1])
    for distance, block in sent.items():
        grad_at[distance] = swapped(block, "ctx", 1)
    grads = key_terms(1, grads, [query_at[reach - 1]])
    grads = key_terms(2, grads)
    keep, *gives = call(
        functools.partial(spread_kernel, step),
        [((1, *chunk), F32)] + [((1, *chunk), BF16)] * (parts - 1),
        [keep, came],
        HINT["part"],
        (),
        [sent[1]],
    )
    shares = [swapped(give, "ctx", (n + 1) * step) for n, give in enumerate(gives)]
    grad_weight, summed = call(
        functools.partial(sum_kernel, 1.0 / math.sqrt(cores * count * tok)),
        [(chunk, F32), ((8, HEAD), F32)],
        [keep, *shares],
        HINT["sum"],
    )
    grads = key_terms(3, grads, [summed, far_query])
    key_grad, value_grad, query_grad = key_terms(4, [*grads, near_query, far_query])
    return (
        output[None],
        grad_weight,
        query_grad[None],
        key_grad[None],
        value_grad[None],
        grad_gates[None],
    )


def solution(mesh):
    rows = P(("groups", "dp"), "ctx", None)
    in_specs = (rows, rows, rows, rows, P(), rows, P(("groups", "dp"), None))
    out_specs = (rows, P(("groups", "ctx", "dp"), None), rows, rows, rows, rows)
    return jax.shard_map(local, mesh=mesh, in_specs=in_specs, out_specs=out_specs, check_vma=False)
```
